32 devices in a mesh: seq: 16 (over z, y, x), tp: 2 (over core).
Axes of the slice: x: 2, y: 2, z: 4, core: 2. Of those that a mesh axis runs over, the one named last changes fastest.
Arguments:
- queries: bfloat16 [16, 32, 4096], P('seq', None, 'tp'), may hold values from -15 to 15
- tree_keys: bfloat16 [16, 32, 1024], P('seq', None, 'tp'), may hold values from -15 to 15
- tree_values: bfloat16 [16, 32, 1024], P('seq', None, 'tp'), may hold values from -6 to 6
- cache_keys: bfloat16 [9216, 1024], P('seq', 'tp'), may hold values from -15 to 15
- cache_values: bfloat16 [9216, 1024], P('seq', 'tp'), may hold values from -6 to 6
- residual: bfloat16 [16, 32, 4096], P('seq', None, 'tp'), may hold values from -6 to 6
- out_weight: bfloat16 [4096, 4096], P('tp'), may hold values from -0.125 to 0.125
- cache_len: int32 [16], replicated, may hold values from 88 to 1720, as said below
- parents: int32 [16, 32], P('seq'), may hold values from -1 to 30, as said below
- accept_rows: int32 [16, 8], P('seq'), may hold values from 0 to 31, as said below
- accept_len: int32 [16], replicated, may hold values from 1 to 8
Outputs:
- mixed: bfloat16 [16, 32, 4096], P('seq', None, 'tp')
- new_cache_keys: bfloat16 [9216, 1024], P('seq', 'tp')
- new_cache_values: bfloat16 [9216, 1024], P('seq', 'tp')
The draws below stay inside these ranges and needn't reach their ends.
Inputs may be any that keep to these rules, and one draw needn't show every extreme that they name: Requests form aligned groups of 4 (requests 4 g to 4 g + 3). Request r owns cache_len[r] + 8 pool positions, these regions follow one another in request order from position 0, and the regions of one group fill exactly 2304 positions, so that group g's caches lie in pool positions 4 * 576 * g to 4 * 576 * (g + 1) - 1. parents[r, 0] = -1, and 0 <= parents[r, i] < i for i > 0. `accept_rows`: entries 0 to accept_len[r] - 1 are a chain of tree tokens that starts at token 0, each entry's parent being the entry before it; later entries are 31 and are not used.
All inputs are finite; a program needn't handle non-finite values.
Results may differ from the reference program's by a relative error of at most 0.009.
Values may be sent and summed in bfloat16 or wider, within the bound.
A program may use at most 64 MiB of HBM per device.

```python
import math
import jax
import jax.numpy as jnp
from jax import lax

D = 4096
HQ = 32
KVH = 8
HD = 128
TREE = 32
A_MAX = 8
GROUP = 4
P_DEV = 576
REQS = 16
POOL = 9216


def drawn_rows(key, leading, heads, salt):
    drawn = jnp.clip(jax.random.normal(jax.random.fold_in(key, salt), leading + (heads, HD), jnp.float32), -6.0, 6.0)
    return drawn.reshape(leading + (heads * HD,))


def draw_queries(key, part):
    values = drawn_rows(key, (REQS, TREE), HQ, 31)
    return values.astype(jnp.bfloat16)


def draw_tree_keys(key, part):
    values = drawn_rows(key, (REQS, TREE), KVH, 41)
    return values.astype(jnp.bfloat16)


def draw_cache_keys(key, part):
    values = drawn_rows(key, (P_DEV * REQS,), KVH, 51)
    return values.astype(jnp.bfloat16)


def draw_cache_len(key, part):
    groups = REQS // GROUP
    long_at = jax.random.randint(jax.random.fold_in(key, 11), (groups, 1), 0, GROUP)
    third = P_DEV // 3
    stride = P_DEV // 12
    first_shift = jax.random.randint(jax.random.fold_in(key, 12), (groups,), -stride, stride + 1)
    second_shift = jax.random.randint(jax.random.fold_in(key, 13), (groups,), -stride, stride + 1)
    picked = jax.random.randint(jax.random.fold_in(key, 14), (), 0, groups)
    group_ids = jnp.arange(groups, dtype=jnp.int32)
    first_shift = jnp.where(group_ids == picked, stride, first_shift)
    second_shift = jnp.where(group_ids == picked, -stride, second_shift)
    shorts = jnp.stack([third + first_shift, third - first_shift + second_shift, third - second_shift], axis=1)
    slots = jnp.arange(GROUP, dtype=jnp.int32)[None, :]
    short_index = jnp.clip(slots - (slots > long_at).astype(jnp.int32), 0, 2)
    short_value = jnp.take_along_axis(shorts, jnp.broadcast_to(short_index, (groups, GROUP)), axis=1)
    regions = jnp.where(slots == long_at, (GROUP - 1) * P_DEV, short_value)
    return (regions - A_MAX).reshape(-1).astype(jnp.int32)


def tree_layout(key):
    members = jnp.arange(TREE, dtype=jnp.int32)
    lowest = jnp.maximum(members - 3, 0)
    highest = jnp.maximum(members, 1)
    parent_ids = jax.random.randint(jax.random.fold_in(key, 21), (REQS, TREE), lowest, highest)
    parent_ids = jnp.where(members[None, :] == 0, -1, parent_ids).astype(jnp.int32)
    parent_ids = parent_ids.at[0, TREE - 1].set(TREE - 2)
    endings = jax.random.randint(jax.random.fold_in(key, 22), (REQS,), 0, TREE)
    order = jax.random.permutation(jax.random.fold_in(key, 23), REQS)
    endings = endings.at[order[0]].set(0).at[order[1]].set(TREE - 1)
    current = endings.astype(jnp.int32)
    links = [current]
    for repeat in range(TREE - 1):
        hopped = jnp.take_along_axis(parent_ids, jnp.maximum(current, 0)[:, None], axis=1)[:, 0]
        current = jnp.where(current >= 0, hopped, -1)
        links.append(current)
    chain = jnp.stack(links, axis=1)
    depth = jnp.sum((chain >= 0).astype(jnp.int32), axis=1) - 1
    counts = jnp.minimum(depth + 1, A_MAX).astype(jnp.int32)
    column = jnp.arange(A_MAX, dtype=jnp.int32)
    picks = jnp.maximum(depth[:, None] - column[None, :], 0)
    path_rows = jnp.take_along_axis(chain, picks, axis=1)
    path_rows = jnp.where(column[None, :] < counts[:, None], path_rows, TREE - 1).astype(jnp.int32)
    return (parent_ids, path_rows, counts)


def draw_parents(key, part):
    return tree_layout(jax.random.fold_in(key, 77))[0]


def draw_accept_rows(key, part):
    return tree_layout(jax.random.fold_in(key, 77))[1]


def draw_accept_len(key, part):
    return tree_layout(jax.random.fold_in(key, 77))[2]


def with_spikes(result, stream_key, source, target, parts, factor):
    def block_of(axis_at):
        return (jnp.arange(result.shape[axis_at]) // (result.shape[axis_at] // parts)).reshape((-1,) + (1,) * (result.ndim - 1 - axis_at))

    first = jax.random.permutation(stream_key, parts)[block_of(target)]
    second = (block_of(target) + parts // 2) % parts
    return jnp.where((block_of(source) == first) | (block_of(source) == second), factor * result, result)


def steps_of(key, extent, split, low, top_value):
    def one(dim, shards_of):
        steps = jax.random.uniform(jax.random.fold_in(jax.random.fold_in(key, 6), dim), (shards_of,), jnp.float32, low / len(split), top_value / len(split))
        return jnp.repeat(jnp.exp(steps), extent[dim] // shards_of).reshape((-1,) + (1,) * (len(extent) - dim - 1))

    loudness = one(*split[0])
    for cut in split[1:]:
        loudness = loudness * one(*cut)
    return loudness


def centred(own_key, shape, width, bound, cuts=(), kind=jnp.bfloat16):
    drawn = jax.random.normal(own_key, shape, jnp.float32) * width
    if len(cuts) > 0:
        drawn = steps_of(own_key, shape, cuts, -0.22, 0.18) * drawn
    return jnp.clip(drawn, min=-bound, max=bound).astype(kind)


def bell_draw_with(rng, dims, deviation, limit, split, heavy, kind=jnp.bfloat16):
    values = deviation * jax.random.normal(rng, dims, jnp.float32)
    if split:
        values = values * steps_of(rng, dims, split, -0.22, 0.18)
    return jnp.clip(with_spikes(values, jax.random.fold_in(rng, 3), *heavy), -limit, limit).astype(kind)


def setup_inputs(seed: int = 0) -> dict:
    arg_keys = jax.random.split(jax.random.key(seed), 12)
    queries = draw_queries(jax.random.fold_in(arg_keys[11], 71), 0)
    tree_keys = draw_tree_keys(jax.random.fold_in(arg_keys[11], 71), 0)
    tree_values = centred(arg_keys[2], (REQS, TREE, KVH * HD), 1.0, 6.0, ((0, 16), (2, 2)))
    cache_keys = draw_cache_keys(jax.random.fold_in(arg_keys[11], 71), 0)
    cache_values = centred(arg_keys[4], (POOL, KVH * HD), 1.0, 6.0, ((0, 16), (1, 2)))
    residual = centred(arg_keys[5], (REQS, TREE, D), 1.0, 6.0, ((0, 16), (2, 2)))
    out_weight = bell_draw_with(arg_keys[6], (HQ * HD, D), (HQ * HD) ** -0.5, 0.125, ((0, 2),), (0, 1, 2, 2.0))
    cache_len = draw_cache_len(jax.random.fold_in(arg_keys[11], 71), 0)
    parents = draw_parents(jax.random.fold_in(arg_keys[11], 71), 0)
    accept_rows = draw_accept_rows(jax.random.fold_in(arg_keys[11], 71), 0)
    accept_len = draw_accept_len(jax.random.fold_in(arg_keys[11], 71), 0)
    return {"queries": queries, "tree_keys": tree_keys, "tree_values": tree_values, "cache_keys": cache_keys, "cache_values": cache_values, "residual": residual, "out_weight": out_weight, "cache_len": cache_len, "parents": parents, "accept_rows": accept_rows, "accept_len": accept_len}


NEG = -1e+30

def ancestry(parents):
    length = parents.shape[-1]
    members = jnp.arange(length, dtype=jnp.int32)
    ancestors = jnp.broadcast_to(members[:, None] == members[None, :], parents.shape + (length,))
    current = parents
    for repeat in range(length - 1):
        ancestors = ancestors | (current[..., None] == members)
        hopped = jnp.take_along_axis(parents, jnp.maximum(current, 0), axis=-1)
        current = jnp.where(current >= 0, hopped, -1)
    return ancestors

def reference(queries, tree_keys, tree_values, cache_keys, cache_values, residual, out_weight, cache_len, parents, accept_rows, accept_len):
    pool_size = cache_keys.shape[0]
    window = min(GROUP * P_DEV, pool_size)
    regions = cache_len + A_MAX
    starts = (jnp.cumsum(regions) - regions).astype(jnp.int32)
    ancestors = ancestry(parents)
    sharing = HQ // KVH
    factor = 1.0 / math.sqrt(HD)
    highest = lax.Precision.HIGHEST

    def attend(request):
        query_rows = queries[request].reshape(TREE, KVH, sharing, HD).astype(jnp.float32)
        begin = starts[request]
        length = cache_len[request]
        offset = jnp.minimum(begin, pool_size - window).astype(jnp.int32)
        keys_win = lax.dynamic_slice_in_dim(cache_keys, offset, window, 0).reshape(window, KVH, HD).astype(jnp.float32)
        values_win = lax.dynamic_slice_in_dim(cache_values, offset, window, 0).reshape(window, KVH, HD).astype(jnp.float32)
        places = offset + jnp.arange(window, dtype=jnp.int32)
        inside = (places >= begin) & (places < begin + length)
        cached = jnp.einsum('tkgd,pkd->kgtp', query_rows, keys_win, precision=highest) * factor
        own_keys = tree_keys[request].reshape(TREE, KVH, HD).astype(jnp.float32)
        own_values = tree_values[request].reshape(TREE, KVH, HD).astype(jnp.float32)
        drafted = jnp.einsum('tkgd,jkd->kgtj', query_rows, own_keys, precision=highest) * factor
        linked = ancestors[request]
        top = jnp.maximum(lax.optimization_barrier(jnp.max(jnp.where(inside, cached, NEG), axis=-1)), lax.optimization_barrier(jnp.max(jnp.where(linked, drafted, NEG), axis=-1)))
        cache_raised = jnp.where(inside, jnp.exp(cached - top[..., None]), 0.0)
        tree_raised = jnp.where(linked, jnp.exp(drafted - top[..., None]), 0.0)
        total = lax.optimization_barrier(jnp.sum(cache_raised, axis=-1)) + lax.optimization_barrier(jnp.sum(tree_raised, axis=-1))
        cache_weights = lax.optimization_barrier(cache_raised.astype(jnp.bfloat16)).astype(jnp.float32)
        tree_weights = lax.optimization_barrier(tree_raised.astype(jnp.bfloat16)).astype(jnp.float32)
        summed = jnp.einsum('kgtp,pkd->tkgd', cache_weights, values_win, precision=highest)
        summed = summed + jnp.einsum('kgtj,jkd->tkgd', tree_weights, own_values, precision=highest)
        scaled = summed / jnp.transpose(total, (2, 0, 1))[..., None]
        return scaled.astype(jnp.bfloat16).reshape(TREE, HQ * HD)
    attention = lax.map(attend, jnp.arange(REQS, dtype=jnp.int32))
    projected = jnp.dot(attention.reshape(REQS * TREE, HQ * HD), out_weight, preferred_element_type=jnp.float32)
    mixed = (residual.astype(jnp.float32) + projected.reshape(REQS, TREE, D)).astype(jnp.bfloat16)
    column = jnp.arange(A_MAX, dtype=jnp.int32)
    targets = starts[:, None] + cache_len[:, None] + column[None, :]
    targets = jnp.where(column[None, :] < accept_len[:, None], targets, pool_size).reshape(-1).astype(jnp.int32)
    key_rows = jnp.take_along_axis(tree_keys, accept_rows[:, :, None], axis=1).reshape(-1, KVH * HD)
    value_rows = jnp.take_along_axis(tree_values, accept_rows[:, :, None], axis=1).reshape(-1, KVH * HD)
    new_cache_keys = cache_keys.at[targets].set(key_rows, mode='drop')
    new_cache_values = cache_values.at[targets].set(value_rows, mode='drop')
    return (mixed, new_cache_keys, new_cache_values)
```

```python
import functools
import math

import jax
import jax.numpy as jnp
from jax import lax
from jax.experimental import pallas as pl
from jax.experimental.pallas import tpu as pltpu
from jax.sharding import PartitionSpec as P

HD = 128
TREE = 32
A_MAX = 8
GROUP = 4
NEG = -1e30
FLOOR = -1e29
TAIL = 16
MESH = pl.DeviceIdType.MESH


def kernel(
    n_tp,
    len_ref,
    acc_len_ref,
    parents_ref,
    accept_ref,
    q_hbm,
    tk_hbm,
    tv_hbm,
    ck_hbm,
    cv_hbm,
    res_hbm,
    w_hbm,
    mixed_ref,
    nk_hbm,
    nv_hbm,
    kbuf,
    vbuf,
    vt,
    qown,
    qbuf,
    bias,
    own_o,
    own_s,
    psend,
    precv,
    rows,
    rrecv,
    wbuf,
    att,
    acc,
    tsend,
    trecv,
    resbuf,
    nk,
    nv,
    loc_sem,
    w_sem,
    out_sem,
    q_ss,
    q_rs,
    p_ss,
    p_rs,
    r_ss,
    r_rs,
    t_ss,
    t_rs,
):
    positions, channels = ck_hbm.shape
    kv = channels // HD
    qk = q_hbm.shape[2] // kv
    sharing = qk // HD
    lanes = sharing * TREE
    span = kbuf.shape[0]
    used = positions + TREE
    w_loc = res_hbm.shape[2]
    scale = math.log2(math.e) / math.sqrt(HD)

    seq = lax.axis_index("seq")
    tp = lax.axis_index("tp")
    base = seq // GROUP * GROUP
    within = seq - base
    low, high = within % 2, within // 2

    def peer_of(d):
        return (low + d % 2) % 2 + 2 * ((high + d // 2) % 2)

    locals_ = [
        pltpu.make_async_copy(tk_hbm.at[0], kbuf.at[pl.ds(positions, TREE)], loc_sem.at[0]),
        pltpu.make_async_copy(tv_hbm.at[0], vbuf.at[pl.ds(positions, TREE)], loc_sem.at[1]),
        pltpu.make_async_copy(q_hbm.at[0], qown, loc_sem.at[2]),
        pltpu.make_async_copy(ck_hbm, kbuf.at[pl.ds(0, positions)], loc_sem.at[3]),
        pltpu.make_async_copy(cv_hbm, vbuf.at[pl.ds(0, positions)], loc_sem.at[4]),
        pltpu.make_async_copy(res_hbm.at[0], resbuf, loc_sem.at[5]),
    ]
    for c in locals_:
        c.start()

    barrier = pltpu.get_barrier_semaphore()
    for d in range(1, GROUP):
        pl.semaphore_signal(barrier, inc=1, device_id=(base + peer_of(d), tp), device_id_type=MESH)
    for d in range(1, n_tp):
        pl.semaphore_signal(barrier, inc=1, device_id=(seq, (tp + d) % n_tp), device_id_type=MESH)
    pl.semaphore_wait(barrier, GROUP - 1 + n_tp - 1)

    def q_copy(d, k):
        return pltpu.make_async_remote_copy(
            src_ref=q_hbm.at[0, :, pl.ds(pl.multiple_of(k * qk, qk), qk)],
            dst_ref=qbuf.at[d - 1, k],
            send_sem=q_ss.at[d - 1, k],
            recv_sem=q_rs.at[d - 1, k],
            device_id=(base + peer_of(d), tp),
            device_id_type=MESH,
        )

    def p_copy(d, k):
        return pltpu.make_async_remote_copy(
            src_ref=psend.at[d - 1, k],
            dst_ref=precv.at[d - 1, k],
            send_sem=p_ss.at[d - 1, k],
            recv_sem=p_rs.at[d - 1, k],
            device_id=(base + peer_of(d), tp),
            device_id_type=MESH,
        )

    def r_copy(d):
        return pltpu.make_async_remote_copy(
            src_ref=rows,
            dst_ref=rrecv.at[d - 1],
            send_sem=r_ss.at[d - 1],
            recv_sem=r_rs.at[d - 1],
            device_id=(base + peer_of(d), tp),
            device_id_type=MESH,
        )

    def t_copy(d):
        return pltpu.make_async_remote_copy(
            src_ref=tsend.at[d - 1],
            dst_ref=trecv.at[d - 1],
            send_sem=t_ss.at[d - 1],
            recv_sem=t_rs.at[d - 1],
            device_id=(seq, (tp + d) % n_tp),
            device_id_type=MESH,
        )

    def w_copy(k):
        rows_k = pl.ds(pl.multiple_of(k * qk, qk), qk)
        return pltpu.make_async_copy(w_hbm.at[rows_k], wbuf.at[rows_k], w_sem.at[k])

    for k in range(kv):
        for d in (1, 2, 3):
            q_copy(d, k).start()
    for k in range(kv):
        w_copy(k).start()

    lens = [len_ref[base + r] for r in range(GROUP)]
    begins = []
    at = -within * positions
    for r in range(GROUP):
        begins.append(at)
        at = at + lens[r] + A_MAX
    place = lax.broadcasted_iota(jnp.int32, (positions, lanes), 0)
    for d in range(GROUP):
        peer = peer_of(d)
        first, size = begins[0], lens[0]
        for r in range(1, GROUP):
            first = jnp.where(peer == r, begins[r], first)
            size = jnp.where(peer == r, lens[r], size)
        inside = (place >= first) & (place < first + size)
        bias[d, pl.ds(0, positions), :] = jnp.where(inside, 0.0, NEG)
        bias[d, pl.ds(positions, span - positions), :] = jnp.full(
            (span - positions, lanes), NEG, jnp.float32
        )

    i32 = jnp.int32
    row_i = lax.broadcasted_iota(i32, (TREE, TREE), 0)
    col_i = lax.broadcasted_iota(i32, (TREE, TREE), 1)
    parents = jnp.broadcast_to(parents_ref[...], (TREE, TREE))
    reach = jnp.where((row_i == col_i) | (parents == row_i), 1.0, 0.0)
    for _ in range((TREE - 1).bit_length()):
        half = reach.astype(jnp.bfloat16)
        reach = jnp.minimum(jnp.dot(half, half, preferred_element_type=jnp.float32), 1.0)
    spread = jnp.where(
        lax.broadcasted_iota(i32, (TREE, lanes), 0)
        == lax.broadcasted_iota(i32, (TREE, lanes), 1) % TREE,
        1.0,
        0.0,
    ).astype(jnp.bfloat16)
    linked = jnp.dot(reach.astype(jnp.bfloat16), spread, preferred_element_type=jnp.float32)
    bias[0, pl.ds(positions, TREE), :] = jnp.where(linked > 0.5, 0.0, NEG)

    if span > used:
        kbuf[pl.ds(used, span - used), :] = jnp.zeros((span - used, channels), jnp.bfloat16)
        vbuf[pl.ds(used, span - used), :] = jnp.zeros((span - used, channels), jnp.bfloat16)

    locals_[0].wait()
    locals_[1].wait()
    chosen = jnp.where(
        jnp.broadcast_to(accept_ref[...], (TREE, A_MAX))
        == lax.broadcasted_iota(i32, (TREE, A_MAX), 0),
        1.0,
        0.0,
    ).astype(jnp.bfloat16)
    dims = (((0,), (0,)), ((), ()))
    tree_rows = pl.ds(positions, TREE)
    rows[...] = jnp.concatenate(
        [
            lax.dot_general(chosen, kbuf[tree_rows, :], dims, preferred_element_type=jnp.float32),
            lax.dot_general(chosen, vbuf[tree_rows, :], dims, preferred_element_type=jnp.float32),
        ],
        axis=0,
    ).astype(jnp.bfloat16)
    for d in range(1, GROUP):
        r_copy(d).start()

    for i in (2, 3, 4):
        locals_[i].wait()
    for k in range(kv):
        vt[k] = vbuf[:, k * HD : (k + 1) * HD].astype(jnp.float32).T.astype(jnp.bfloat16)

    def attend(queries, k, which):
        stacked = jnp.concatenate(
            [queries[:, g * HD : (g + 1) * HD] for g in range(sharing)], axis=0
        )
        keys = kbuf[:, pl.ds(pl.multiple_of(k * HD, HD), HD)]
        scores = lax.dot_general(
            keys, stacked, (((1,), (1,)), ((), ())), preferred_element_type=jnp.float32
        )
        scores = scores + bias[which]
        top = jnp.maximum(jnp.max(scores, axis=0, keepdims=True), FLOOR)
        top = top.astype(jnp.bfloat16).astype(jnp.float32)
        raised = jnp.exp2((scores - top) * scale)
        total = jnp.sum(raised, axis=0, keepdims=True)
        out = jnp.dot(vt[k], raised.astype(jnp.bfloat16), preferred_element_type=jnp.float32)
        return out, top, total

    def own_step(k, carry):
        out, top, total = attend(qown[:, pl.ds(pl.multiple_of(k * qk, qk), qk)], k, 0)
        own_o[k] = out
        own_s[k] = jnp.concatenate(
            [top, total, jnp.zeros((6, lanes), jnp.float32)], axis=0
        )
        return carry

    lax.fori_loop(0, kv, own_step, 0)

    tail_row = lax.broadcasted_iota(i32, (TAIL, lanes), 0)

    def peer_step(k, carry):
        for d in (1, 2, 3):
            q_copy(d, k).wait_recv()
            out, top, total = attend(qbuf[d - 1, k], k, d)
            psend[d - 1, k, pl.ds(0, HD), :] = out.astype(jnp.bfloat16)
            main = total.astype(jnp.bfloat16).astype(jnp.float32)
            tail = jnp.where(
                tail_row == 0, top, jnp.where(tail_row == 1, main, total - main)
            )
            psend[d - 1, k, pl.ds(HD, TAIL), :] = tail.astype(jnp.bfloat16)
            p_copy(d, k).start()
        return carry

    lax.fori_loop(0, kv, peer_step, 0)

    for d in range(1, GROUP):
        r_copy(d).wait_recv()
    wide = GROUP * 2 * A_MAX
    col = lax.broadcasted_iota(i32, (1, wide), 1)
    slot = col % (2 * A_MAX)
    targets = jnp.full((1, wide), -1, i32)
    for d in range(GROUP):
        peer = peer_of(d)
        end, taken = begins[0] + lens[0], acc_len_ref[base]
        for r in range(1, GROUP):
            end = jnp.where(peer == r, begins[r] + lens[r], end)
            taken = jnp.where(peer == r, acc_len_ref[base + r], taken)
        hit = (col // (2 * A_MAX) == d) & (slot % A_MAX < taken)
        targets = jnp.where(hit, end + slot % A_MAX, targets)
    arrived = jnp.concatenate([rows[...]] + [rrecv[d] for d in range(GROUP - 1)], axis=0)
    where_row = lax.broadcasted_iota(i32, (positions, wide), 0)
    outs = []
    for half, (old, new, dest) in enumerate(((kbuf, nk, nk_hbm), (vbuf, nv, nv_hbm))):
        mine = jnp.where(slot // A_MAX == half, targets, -1)
        pick = jnp.where(where_row == mine, 1.0, 0.0)
        changed = jnp.max(pick, axis=1, keepdims=True)
        put = jnp.dot(pick.astype(jnp.bfloat16), arrived, preferred_element_type=jnp.float32)
        new[...] = jnp.where(changed > 0.5, put, old[pl.ds(0, positions), :].astype(jnp.float32)).astype(
            jnp.bfloat16
        )
        copy = pltpu.make_async_copy(new, dest, out_sem.at[half])
        copy.start()
        outs.append(copy)

    def gather(k):
        tops = [own_s[k, pl.ds(0, 1), :]]
        totals = [own_s[k, pl.ds(1, 1), :]]
        parts = [own_o[k]]
        for d in (1, 2, 3):
            p_copy(d, k).wait_recv()
            tail = precv[d - 1, k, pl.ds(HD, TAIL), :].astype(jnp.float32)
            tops.append(tail[0:1])
            totals.append(tail[1:2] + tail[2:3])
            parts.append(precv[d - 1, k, pl.ds(0, HD), :].astype(jnp.float32))
        top = functools.reduce(jnp.maximum, tops)
        factors = [jnp.exp2((t - top) * scale) for t in tops]
        total = sum(f * t for f, t in zip(factors, totals))
        out = sum(f * p for f, p in zip(factors, parts)) * (1.0 / total)
        turned = out.T.astype(jnp.bfloat16)
        for g in range(sharing):
            att[:, g * HD : (g + 1) * HD] = turned[g * TREE : (g + 1) * TREE]

    step = min(w_loc, 1024)

    def project(k, d):
        peer = (tp + d) % n_tp
        left = att[...]
        for c in range(w_loc // step):
            columns = pl.ds(pl.multiple_of(peer * w_loc + c * step, HD), step)
            part = jnp.dot(
                left,
                wbuf[pl.ds(pl.multiple_of(k * qk, qk), qk), columns],
                preferred_element_type=jnp.float32,
            )
            acc[d, :, c * step : (c + 1) * step] += part

    acc[...] = jnp.zeros_like(acc)

    def out_step(k, carry):
        w_copy(k).wait()
        gather(k)
        for d in range(n_tp):
            project(k, d)
        return carry

    lax.fori_loop(0, kv - 1, out_step, 0)
    w_copy(kv - 1).wait()
    gather(kv - 1)
    for d in range(1, n_tp):
        project(kv - 1, d)
        tsend[d - 1] = acc[d].astype(jnp.bfloat16)
        t_copy(d).start()
    project(kv - 1, 0)
    locals_[5].wait()
    result = acc[0] + resbuf[...].astype(jnp.float32)
    for d in range(1, n_tp):
        t_copy(d).wait_recv()
        result = result + trecv[d - 1].astype(jnp.float32)
    mixed_ref[0] = result.astype(jnp.bfloat16)

    for copy in outs:
        copy.wait()
    for d in range(1, GROUP):
        r_copy(d).wait_send()
        for k in range(kv):
            q_copy(d, k).wait_send()
            p_copy(d, k).wait_send()
    for d in range(1, n_tp):
        t_copy(d).wait_send()


def on_device(n_tp, queries, tree_keys, tree_values, cache_keys, cache_values, residual, out_weight, cache_len, parents, accept_rows, accept_len):
    positions, channels = cache_keys.shape
    kv = channels // HD
    q_width = queries.shape[2]
    qk = q_width // kv
    lanes = qk // HD * TREE
    w_loc = residual.shape[2]
    span = -(-(positions + TREE) // 128) * 128
    bf16, f32 = jnp.bfloat16, jnp.float32
    peers = GROUP - 1
    vmem = pltpu.VMEM
    dma = pltpu.SemaphoreType.DMA
    hbm = pl.BlockSpec(memory_space=pl.ANY)
    smem = pl.BlockSpec(memory_space=pltpu.SMEM)
    local = pl.BlockSpec(memory_space=pltpu.VMEM)
    return pl.pallas_call(
        functools.partial(kernel, n_tp),
        out_shape=(
            jax.ShapeDtypeStruct(residual.shape, bf16),
            jax.ShapeDtypeStruct(cache_keys.shape, bf16),
            jax.ShapeDtypeStruct(cache_values.shape, bf16),
        ),
        in_specs=[smem, smem, local, local] + [hbm] * 7,
        out_specs=(local, hbm, hbm),
        scratch_shapes=[
            vmem((span, channels), bf16),
            vmem((span, channels), bf16),
            vmem((kv, HD, span), bf16),
            vmem((TREE, q_width), bf16),
            vmem((peers, kv, TREE, qk), bf16),
            vmem((GROUP, span, lanes), f32),
            vmem((kv, HD, lanes), f32),
            vmem((kv, 8, lanes), f32),
            vmem((peers, kv, HD + TAIL, lanes), bf16),
            vmem((peers, kv, HD + TAIL, lanes), bf16),
            vmem((2 * A_MAX, channels), bf16),
            vmem((peers, 2 * A_MAX, channels), bf16),
            vmem(out_weight.shape, bf16),
            vmem((TREE, qk), bf16),
            vmem((n_tp, TREE, w_loc), f32),
            vmem((max(n_tp - 1, 1), TREE, w_loc), bf16),
            vmem((max(n_tp - 1, 1), TREE, w_loc), bf16),
            vmem((TREE, w_loc), bf16),
            vmem((positions, channels), bf16),
            vmem((positions, channels), bf16),
            dma((6,)),
            dma((kv,)),
            dma((2,)),
            dma((peers, kv)),
            dma((peers, kv)),
            dma((peers, kv)),
            dma((peers, kv)),
            dma((peers,)),
            dma((peers,)),
            dma((max(n_tp - 1, 1),)),
            dma((max(n_tp - 1, 1),)),
        ],
        compiler_params=pltpu.CompilerParams(
            collective_id=0, has_side_effects=True, vmem_limit_bytes=48 * 1024 * 1024
        ),
        name="tree_attention",
    )(cache_len, accept_len, parents, accept_rows, queries, tree_keys, tree_values, cache_keys, cache_values, residual, out_weight)


def solution(mesh):
    return jax.shard_map(
        functools.partial(on_device, mesh.shape["tp"]),
        mesh=mesh,
        in_specs=(
            P("seq", None, "tp"),
            P("seq", None, "tp"),
            P("seq", None, "tp"),
            P("seq", "tp"),
            P("seq", "tp"),
            P("seq", None, "tp"),
            P("tp", None),
            P(),
            P("seq", None),
            P("seq", None),
            P(),
        ),
        out_specs=(P("seq", None, "tp"), P("seq", "tp"), P("seq", "tp")),
        check_vma=False,
    )
```

```python
import functools
import math

import jax
import jax.numpy as jnp
from jax import lax
from jax.experimental import pallas as pl
from jax.experimental.pallas import tpu as pltpu
from jax.sharding import PartitionSpec as P

HD = 128
TREE = 32
A_MAX = 8
GROUP = 4
NEG = -1e30
FLOOR = -1e29
TAIL = 16
CUTS = 4
MESH = pl.DeviceIdType.MESH


def kernel(
    n_tp,
    len_hbm,
    acc_len_hbm,
    parents_hbm,
    accept_hbm,
    q_hbm,
    tk_hbm,
    tv_hbm,
    ck_hbm,
    cv_hbm,
    res_hbm,
    w_hbm,
    mixed_ref,
    nk_hbm,
    nv_hbm,
    len_ref,
    acc_len_ref,
    parents_ref,
    accept_ref,
    kbuf,
    vbuf,
    vt,
    qown,
    qbuf,
    bias,
    own_o,
    own_s,
    psend,
    precv,
    rows,
    rrecv,
    wbuf,
    att,
    acc,
    tsend,
    trecv,
    resbuf,
    nk,
    nv,
    loc_sem,
    w_sem,
    out_sem,
    q_ss,
    q_rs,
    p_ss,
    p_rs,
    r_ss,
    r_rs,
    t_ss,
    t_rs,
):
    positions, channels = ck_hbm.shape
    kv = channels // HD
    qk = q_hbm.shape[2] // kv
    sharing = qk // HD
    lanes = sharing * TREE
    span = kbuf.shape[0]
    used = positions + TREE
    w_loc = res_hbm.shape[2]
    scale = math.log2(math.e) / math.sqrt(HD)

    seq = lax.axis_index("seq")
    tp = lax.axis_index("tp")
    base = seq // GROUP * GROUP
    within = seq - base
    low, high = within % 2, within // 2

    def peer_of(d):
        return (low + d % 2) % 2 + 2 * ((high + d // 2) % 2)

    barrier = pltpu.get_barrier_semaphore()
    for d in range(1, GROUP):
        pl.semaphore_signal(barrier, inc=1, device_id=(base + peer_of(d), tp), device_id_type=MESH)
    for d in range(1, n_tp):
        pl.semaphore_signal(barrier, inc=1, device_id=(seq, (tp + d) % n_tp), device_id_type=MESH)
    locals_ = [
        pltpu.make_async_copy(tk_hbm.at[0], kbuf.at[pl.ds(positions, TREE)], loc_sem.at[0]),
        pltpu.make_async_copy(tv_hbm.at[0], vbuf.at[pl.ds(positions, TREE)], loc_sem.at[1]),
        pltpu.make_async_copy(q_hbm.at[0], qown, loc_sem.at[2]),
        pltpu.make_async_copy(ck_hbm, kbuf.at[pl.ds(0, positions)], loc_sem.at[3]),
        pltpu.make_async_copy(cv_hbm, vbuf.at[pl.ds(0, positions)], loc_sem.at[4]),
        pltpu.make_async_copy(res_hbm.at[0], resbuf, loc_sem.at[5]),
        pltpu.make_async_copy(len_hbm, len_ref, loc_sem.at[6]),
        pltpu.make_async_copy(acc_len_hbm, acc_len_ref, loc_sem.at[7]),
        pltpu.make_async_copy(parents_hbm, parents_ref, loc_sem.at[8]),
        pltpu.make_async_copy(accept_hbm, accept_ref, loc_sem.at[9]),
    ]
    for c in locals_:
        c.start()

    pl.semaphore_wait(barrier, GROUP - 1 + n_tp - 1)

    def q_copy(d, k):
        return pltpu.make_async_remote_copy(
            src_ref=q_hbm.at[0, :, pl.ds(pl.multiple_of(k * qk, qk), qk)],
            dst_ref=qbuf.at[d - 1, k],
            send_sem=q_ss.at[d - 1, k],
            recv_sem=q_rs.at[d - 1, k],
            device_id=(base + peer_of(d), tp),
            device_id_type=MESH,
        )

    def p_copy(d, k):
        return pltpu.make_async_remote_copy(
            src_ref=psend.at[d - 1, k],
            dst_ref=precv.at[d - 1, k],
            send_sem=p_ss.at[d - 1, k],
            recv_sem=p_rs.at[d - 1, k],
            device_id=(base + peer_of(d), tp),
            device_id_type=MESH,
        )

    def r_copy(d):
        return pltpu.make_async_remote_copy(
            src_ref=rows,
            dst_ref=rrecv.at[d - 1],
            send_sem=r_ss.at[d - 1],
            recv_sem=r_rs.at[d - 1],
            device_id=(base + peer_of(d), tp),
            device_id_type=MESH,
        )

    def t_copy(d):
        return pltpu.make_async_remote_copy(
            src_ref=tsend.at[d - 1],
            dst_ref=trecv.at[d - 1],
            send_sem=t_ss.at[d - 1],
            recv_sem=t_rs.at[d - 1],
            device_id=(seq, (tp + d) % n_tp),
            device_id_type=MESH,
        )

    def w_copy(k):
        rows_k = pl.ds(pl.multiple_of(k * qk, qk), qk)
        return pltpu.make_async_copy(w_hbm.at[rows_k], wbuf.at[rows_k], w_sem.at[k])

    for k in range(kv):
        for d in (3, 1, 2):
            q_copy(d, k).start()
    for k in range(kv):
        w_copy(k).start()

    for i in (6, 7, 8, 9):
        locals_[i].wait()

    lens = [len_ref[base + r] for r in range(GROUP)]
    begins = []
    at = -within * positions
    for r in range(GROUP):
        begins.append(at)
        at = at + lens[r] + A_MAX
    place = lax.broadcasted_iota(jnp.int32, (positions, lanes), 0)
    for d in range(GROUP):
        peer = peer_of(d)
        first, size = begins[0], lens[0]
        for r in range(1, GROUP):
            first = jnp.where(peer == r, begins[r], first)
            size = jnp.where(peer == r, lens[r], size)
        inside = (place >= first) & (place < first + size)
        bias[d, pl.ds(0, positions), :] = jnp.where(inside, 0.0, NEG)
        bias[d, pl.ds(positions, span - positions), :] = jnp.full(
            (span - positions, lanes), NEG, jnp.float32
        )

    i32 = jnp.int32
    row_i = lax.broadcasted_iota(i32, (TREE, TREE), 0)
    col_i = lax.broadcasted_iota(i32, (TREE, TREE), 1)
    parents = jnp.broadcast_to(parents_ref[...], (TREE, TREE))
    reach = jnp.where((row_i == col_i) | (parents == row_i), 1.0, 0.0)
    for _ in range((TREE - 1).bit_length()):
        half = reach.astype(jnp.bfloat16)
        reach = jnp.minimum(jnp.dot(half, half, preferred_element_type=jnp.float32), 1.0)
    spread = jnp.where(
        lax.broadcasted_iota(i32, (TREE, lanes), 0)
        == lax.broadcasted_iota(i32, (TREE, lanes), 1) % TREE,
        1.0,
        0.0,
    ).astype(jnp.bfloat16)
    linked = jnp.dot(reach.astype(jnp.bfloat16), spread, preferred_element_type=jnp.float32)
    bias[0, pl.ds(positions, TREE), :] = jnp.where(linked > 0.5, 0.0, NEG)

    if span > used:
        kbuf[pl.ds(used, span - used), :] = jnp.zeros((span - used, channels), jnp.bfloat16)
        vbuf[pl.ds(used, span - used), :] = jnp.zeros((span - used, channels), jnp.bfloat16)

    locals_[0].wait()
    locals_[1].wait()
    chosen = jnp.where(
        jnp.broadcast_to(accept_ref[...], (TREE, A_MAX))
        == lax.broadcasted_iota(i32, (TREE, A_MAX), 0),
        1.0,
        0.0,
    ).astype(jnp.bfloat16)
    dims = (((0,), (0,)), ((), ()))
    tree_rows = pl.ds(positions, TREE)
    rows[...] = jnp.concatenate(
        [
            lax.dot_general(chosen, kbuf[tree_rows, :], dims, preferred_element_type=jnp.float32),
            lax.dot_general(chosen, vbuf[tree_rows, :], dims, preferred_element_type=jnp.float32),
        ],
        axis=0,
    ).astype(jnp.bfloat16)
    for d in range(1, GROUP):
        r_copy(d).start()

    for i in (2, 3, 4):
        locals_[i].wait()
    for k in range(kv):
        vt[k] = vbuf[:, k * HD : (k + 1) * HD].astype(jnp.float32).T.astype(jnp.bfloat16)

    def attend(queries, k, which):
        stacked = jnp.concatenate(
            [queries[:, g * HD : (g + 1) * HD] for g in range(sharing)], axis=0
        )
        keys = kbuf[:, pl.ds(pl.multiple_of(k * HD, HD), HD)]
        scores = lax.dot_general(
            keys, stacked, (((1,), (1,)), ((), ())), preferred_element_type=jnp.float32
        )
        scores = scores + bias[which]
        top = jnp.maximum(jnp.max(scores, axis=0, keepdims=True), FLOOR)
        top = top.astype(jnp.bfloat16).astype(jnp.float32)
        raised = jnp.exp2((scores - top) * scale)
        total = jnp.sum(raised, axis=0, keepdims=True)
        out = jnp.dot(vt[k], raised.astype(jnp.bfloat16), preferred_element_type=jnp.float32)
        return out, top, total

    def own_step(k, carry):
        out, top, total = attend(qown[:, pl.ds(pl.multiple_of(k * qk, qk), qk)], k, 0)
        own_o[k] = out
        own_s[k] = jnp.concatenate(
            [top, total, jnp.zeros((6, lanes), jnp.float32)], axis=0
        )
        return carry


    tail_row = lax.broadcasted_iota(i32, (TAIL, lanes), 0)

    def peer_step(k, carry):
        for d in (1, 2, 3):
            q_copy(d, k).wait_recv()
        found = [attend(qbuf[d - 1, k], k, d) for d in (1, 2, 3)]
        for d, (out, top, total) in zip((1, 2, 3), found):
            psend[d - 1, k, pl.ds(0, HD), :] = out.astype(jnp.bfloat16)
            main = total.astype(jnp.bfloat16).astype(jnp.float32)
            tail = jnp.where(
                tail_row == 0, top, jnp.where(tail_row == 1, main, total - main)
            )
            psend[d - 1, k, pl.ds(HD, TAIL), :] = tail.astype(jnp.bfloat16)
        for d in (3, 1, 2):
            p_copy(d, k).start()
        return carry

    lax.fori_loop(0, kv, peer_step, 0)
    lax.fori_loop(0, kv, own_step, 0)

    for d in range(1, GROUP):
        r_copy(d).wait_recv()
    wide = GROUP * 2 * A_MAX
    col = lax.broadcasted_iota(i32, (1, wide), 1)
    slot = col % (2 * A_MAX)
    targets = jnp.full((1, wide), -1, i32)
    for d in range(GROUP):
        peer = peer_of(d)
        end, taken = begins[0] + lens[0], acc_len_ref[base]
        for r in range(1, GROUP):
            end = jnp.where(peer == r, begins[r] + lens[r], end)
            taken = jnp.where(peer == r, acc_len_ref[base + r], taken)
        hit = (col // (2 * A_MAX) == d) & (slot % A_MAX < taken)
        targets = jnp.where(hit, end + slot % A_MAX, targets)
    arrived = jnp.concatenate([rows[...]] + [rrecv[d] for d in range(GROUP - 1)], axis=0)
    where_row = lax.broadcasted_iota(i32, (positions, wide), 0)
    outs = []
    for half, (old, new, dest) in enumerate(((kbuf, nk, nk_hbm), (vbuf, nv, nv_hbm))):
        mine = jnp.where(slot // A_MAX == half, targets, -1)
        pick = jnp.where(where_row == mine, 1.0, 0.0)
        changed = jnp.max(pick, axis=1, keepdims=True)
        put = jnp.dot(pick.astype(jnp.bfloat16), arrived, preferred_element_type=jnp.float32)
        new[...] = jnp.where(changed > 0.5, put, old[pl.ds(0, positions), :].astype(jnp.float32)).astype(
            jnp.bfloat16
        )
        copy = pltpu.make_async_copy(new, dest, out_sem.at[half])
        copy.start()
        outs.append(copy)

    def gather(k):
        tops = [own_s[k, pl.ds(0, 1), :]]
        totals = [own_s[k, pl.ds(1, 1), :]]
        parts = [own_o[k]]
        for d in (1, 2, 3):
            p_copy(d, k).wait_recv()
            tail = precv[d - 1, k, pl.ds(HD, TAIL), :].astype(jnp.float32)
            tops.append(tail[0:1])
            totals.append(tail[1:2] + tail[2:3])
            parts.append(precv[d - 1, k, pl.ds(0, HD), :].astype(jnp.float32))
        top = functools.reduce(jnp.maximum, tops)
        factors = [jnp.exp2((t - top) * scale) for t in tops]
        total = sum(f * t for f, t in zip(factors, totals))
        out = sum(f * p for f, p in zip(factors, parts)) * (1.0 / total)
        turned = out.T.astype(jnp.bfloat16)
        for g in range(sharing):
            att[:, g * HD : (g + 1) * HD] = turned[g * TREE : (g + 1) * TREE]

    step = min(w_loc, 1024)

    def project(k, d):
        peer = (tp + d) % n_tp
        left = att[...]
        for c in range(w_loc // step):
            columns = pl.ds(pl.multiple_of(peer * w_loc + c * step, HD), step)
            part = jnp.dot(
                left,
                wbuf[pl.ds(pl.multiple_of(k * qk, qk), qk), columns],
                preferred_element_type=jnp.float32,
            )
            acc[d, :, c * step : (c + 1) * step] += part

    acc[...] = jnp.zeros_like(acc)

    def out_step(k, carry):
        w_copy(k).wait()
        gather(k)
        for d in range(n_tp):
            project(k, d)
        return carry

    lax.fori_loop(0, kv - 1, out_step, 0)
    w_copy(kv - 1).wait()
    gather(kv - 1)
    for d in range(1, n_tp):
        project(kv - 1, d)
        tsend[d - 1] = acc[d].astype(jnp.bfloat16)
        t_copy(d).start()
    project(kv - 1, 0)
    locals_[5].wait()
    result = acc[0] + resbuf[...].astype(jnp.float32)
    for d in range(1, n_tp):
        t_copy(d).wait_recv()
        result = result + trecv[d - 1].astype(jnp.float32)
    mixed_ref[0] = result.astype(jnp.bfloat16)

    for copy in outs:
        copy.wait()
    for d in range(1, GROUP):
        r_copy(d).wait_send()
        for k in range(kv):
            q_copy(d, k).wait_send()
            p_copy(d, k).wait_send()
    for d in range(1, n_tp):
        t_copy(d).wait_send()


def write_out(a, b, c, a_out, b_out, c_out, sem):
    copies = []
    part = b.shape[0] // CUTS
    for src, dst in ((b, b_out), (c, c_out)):
        for i in range(CUTS):
            rows = pl.ds(i * part, part)
            copies.append((src.at[rows], dst.at[rows]))
    copies.append((a, a_out))
    copies = [pltpu.make_async_copy(x, y, sem.at[i]) for i, (x, y) in enumerate(copies)]
    for copy in copies:
        copy.start()
    for copy in copies:
        copy.wait()


def on_device(n_tp, queries, tree_keys, tree_values, cache_keys, cache_values, residual, out_weight, cache_len, parents, accept_rows, accept_len):
    positions, channels = cache_keys.shape
    kv = channels // HD
    q_width = queries.shape[2]
    qk = q_width // kv
    lanes = qk // HD * TREE
    w_loc = residual.shape[2]
    span = -(-(positions + TREE) // 128) * 128
    bf16, f32 = jnp.bfloat16, jnp.float32
    peers = GROUP - 1
    vmem = pltpu.VMEM
    dma = pltpu.SemaphoreType.DMA
    hbm = pl.BlockSpec(memory_space=pltpu.HBM)
    local = pl.BlockSpec(memory_space=pltpu.VMEM)
    results = (
        jax.ShapeDtypeStruct(residual.shape, bf16),
        jax.ShapeDtypeStruct(cache_keys.shape, bf16),
        jax.ShapeDtypeStruct(cache_values.shape, bf16),
    )
    made = pl.pallas_call(
        functools.partial(kernel, n_tp),
        out_shape=results,
        in_specs=[hbm] * 11,
        out_specs=(local, hbm, hbm),
        scratch_shapes=[
            pltpu.SMEM(cache_len.shape, jnp.int32),
            pltpu.SMEM(accept_len.shape, jnp.int32),
            vmem(parents.shape, jnp.int32),
            vmem(accept_rows.shape, jnp.int32),
            vmem((span, channels), bf16),
            vmem((span, channels), bf16),
            vmem((kv, HD, span), bf16),
            vmem((TREE, q_width), bf16),
            vmem((peers, kv, TREE, qk), bf16),
            vmem((GROUP, span, lanes), f32),
            vmem((kv, HD, lanes), f32),
            vmem((kv, 8, lanes), f32),
            vmem((peers, kv, HD + TAIL, lanes), bf16),
            vmem((peers, kv, HD + TAIL, lanes), bf16),
            vmem((2 * A_MAX, channels), bf16),
            vmem((peers, 2 * A_MAX, channels), bf16),
            vmem(out_weight.shape, bf16),
            vmem((TREE, qk), bf16),
            vmem((n_tp, TREE, w_loc), f32),
            vmem((max(n_tp - 1, 1), TREE, w_loc), bf16),
            vmem((max(n_tp - 1, 1), TREE, w_loc), bf16),
            vmem((TREE, w_loc), bf16),
            vmem((positions, channels), bf16),
            vmem((positions, channels), bf16),
            dma((10,)),
            dma((kv,)),
            dma((2,)),
            dma((peers, kv)),
            dma((peers, kv)),
            dma((peers, kv)),
            dma((peers, kv)),
            dma((peers,)),
            dma((peers,)),
            dma((max(n_tp - 1, 1),)),
            dma((max(n_tp - 1, 1),)),
        ],
        compiler_params=pltpu.CompilerParams(
            collective_id=0, has_side_effects=True, vmem_limit_bytes=62 * 1024 * 1024
        ),
        name="tree_attention",
    )(cache_len, accept_len, parents, accept_rows, queries, tree_keys, tree_values, cache_keys, cache_values, residual, out_weight)
    return pl.pallas_call(
        write_out,
        out_shape=results,
        in_specs=[hbm] * 3,
        out_specs=(hbm, hbm, hbm),
        scratch_shapes=[dma((2 * CUTS + 1,))],
        compiler_params=pltpu.CompilerParams(vmem_limit_bytes=62 * 1024 * 1024),
        name="write_out",
    )(*made)


def solution(mesh):
    return jax.shard_map(
        functools.partial(on_device, mesh.shape["tp"]),
        mesh=mesh,
        in_specs=(
            P("seq", None, "tp"),
            P("seq", None, "tp"),
            P("seq", None, "tp"),
            P("seq", "tp"),
            P("seq", "tp"),
            P("seq", None, "tp"),
            P("tp", None),
            P(),
            P("seq", None),
            P("seq", None),
            P(),
        ),
        out_specs=(P("seq", None, "tp"), P("seq", "tp"), P("seq", "tp")),
        check_vma=False,
    )
```

```python
import functools
import math

import jax
import jax.numpy as jnp
from jax import lax
from jax.experimental import pallas as pl
from jax.experimental.pallas import tpu as pltpu
from jax.sharding import PartitionSpec as P

HD = 128
TREE = 32
A_MAX = 8
GROUP = 4
NEG = -1e30
FLOOR = -1e29
TAIL = 16
CUTS = 3
MESH = pl.DeviceIdType.MESH


def kernel(
    n_tp,
    len_hbm,
    acc_len_hbm,
    parents_hbm,
    accept_hbm,
    q_hbm,
    tk_hbm,
    tv_hbm,
    ck_hbm,
    cv_hbm,
    res_hbm,
    w_hbm,
    mixed_ref,
    nk_hbm,
    nv_hbm,
    len_ref,
    acc_len_ref,
    parents_ref,
    accept_ref,
    kbuf,
    vbuf,
    vt,
    qown,
    qbuf,
    bias,
    own_o,
    own_s,
    psend,
    precv,
    rows,
    rrecv,
    wbuf,
    att,
    acc,
    tsend,
    trecv,
    resbuf,
    nk,
    nv,
    loc_sem,
    w_sem,
    out_sem,
    q_ss,
    q_rs,
    p_ss,
    p_rs,
    r_ss,
    r_rs,
    t_ss,
    t_rs,
):
    positions, channels = ck_hbm.shape
    kv = channels // HD
    qk = q_hbm.shape[2] // kv
    sharing = qk // HD
    lanes = sharing * TREE
    span = kbuf.shape[0]
    used = positions + TREE
    w_loc = res_hbm.shape[2]
    scale = math.log2(math.e) / math.sqrt(HD)

    seq = lax.axis_index("seq")
    tp = lax.axis_index("tp")
    base = seq // GROUP * GROUP
    within = seq - base
    low, high = within % 2, within // 2

    def peer_of(d):
        return (low + d % 2) % 2 + 2 * ((high + d // 2) % 2)

    barrier = pltpu.get_barrier_semaphore()
    for d in range(1, GROUP):
        pl.semaphore_signal(barrier, inc=1, device_id=(base + peer_of(d), tp), device_id_type=MESH)
    for d in range(1, n_tp):
        pl.semaphore_signal(barrier, inc=1, device_id=(seq, (tp + d) % n_tp), device_id_type=MESH)
    locals_ = [
        pltpu.make_async_copy(tk_hbm.at[0], kbuf.at[pl.ds(positions, TREE)], loc_sem.at[0]),
        pltpu.make_async_copy(tv_hbm.at[0], vbuf.at[pl.ds(positions, TREE)], loc_sem.at[1]),
        pltpu.make_async_copy(q_hbm.at[0], qown, loc_sem.at[2]),
        pltpu.make_async_copy(ck_hbm, kbuf.at[pl.ds(0, positions)], loc_sem.at[3]),
        pltpu.make_async_copy(cv_hbm, vbuf.at[pl.ds(0, positions)], loc_sem.at[4]),
        pltpu.make_async_copy(res_hbm.at[0], resbuf, loc_sem.at[5]),
        pltpu.make_async_copy(len_hbm, len_ref, loc_sem.at[6]),
        pltpu.make_async_copy(acc_len_hbm, acc_len_ref, loc_sem.at[7]),
        pltpu.make_async_copy(parents_hbm, parents_ref, loc_sem.at[8]),
        pltpu.make_async_copy(accept_hbm, accept_ref, loc_sem.at[9]),
    ]
    for c in locals_:
        c.start()

    pl.semaphore_wait(barrier, GROUP - 1 + n_tp - 1)

    def q_copy(d, k):
        return pltpu.make_async_remote_copy(
            src_ref=q_hbm.at[0, :, pl.ds(pl.multiple_of(k * qk, qk), qk)],
            dst_ref=qbuf.at[d - 1, k],
            send_sem=q_ss.at[d - 1, k],
            recv_sem=q_rs.at[d - 1, k],
            device_id=(base + peer_of(d), tp),
            device_id_type=MESH,
        )

    def forward(k, via):
        return pltpu.make_async_remote_copy(
            src_ref=qbuf.at[2 - via, k],
            dst_ref=qbuf.at[2, k],
            send_sem=q_ss.at[2, k],
            recv_sem=q_rs.at[2, k],
            device_id=(base + peer_of(via), tp),
            device_id_type=MESH,
        )

    def p_copy(d, k):
        return pltpu.make_async_remote_copy(
            src_ref=psend.at[d - 1, k],
            dst_ref=precv.at[d - 1, k],
            send_sem=p_ss.at[d - 1, k],
            recv_sem=p_rs.at[d - 1, k],
            device_id=(base + peer_of(d), tp),
            device_id_type=MESH,
        )

    def r_copy(d):
        return pltpu.make_async_remote_copy(
            src_ref=rows,
            dst_ref=rrecv.at[d - 1],
            send_sem=r_ss.at[d - 1],
            recv_sem=r_rs.at[d - 1],
            device_id=(base + peer_of(d), tp),
            device_id_type=MESH,
        )

    def t_copy(d):
        return pltpu.make_async_remote_copy(
            src_ref=tsend.at[d - 1],
            dst_ref=trecv.at[d - 1],
            send_sem=t_ss.at[d - 1],
            recv_sem=t_rs.at[d - 1],
            device_id=(seq, (tp + d) % n_tp),
            device_id_type=MESH,
        )

    def w_copy(k):
        rows_k = pl.ds(pl.multiple_of(k * qk, qk), qk)
        return pltpu.make_async_copy(w_hbm.at[rows_k], wbuf.at[rows_k], w_sem.at[k])

    for k in range(kv):
        for d in (1, 2):
            q_copy(d, k).start()
    for k in range(kv):
        w_copy(k).start()

    for i in (6, 7, 8, 9):
        locals_[i].wait()

    lens = [len_ref[base + r] for r in range(GROUP)]
    begins = []
    at = -within * positions
    for r in range(GROUP):
        begins.append(at)
        at = at + lens[r] + A_MAX
    place = lax.broadcasted_iota(jnp.int32, (positions, lanes), 0)
    for d in range(GROUP):
        peer = peer_of(d)
        first, size = begins[0], lens[0]
        for r in range(1, GROUP):
            first = jnp.where(peer == r, begins[r], first)
            size = jnp.where(peer == r, lens[r], size)
        inside = (place >= first) & (place < first + size)
        bias[d, pl.ds(0, positions), :] = jnp.where(inside, 0.0, NEG)
        bias[d, pl.ds(positions, span - positions), :] = jnp.full(
            (span - positions, lanes), NEG, jnp.float32
        )

    i32 = jnp.int32
    row_i = lax.broadcasted_iota(i32, (TREE, TREE), 0)
    col_i = lax.broadcasted_iota(i32, (TREE, TREE), 1)
    parents = jnp.broadcast_to(parents_ref[...], (TREE, TREE))
    reach = jnp.where((row_i == col_i) | (parents == row_i), 1.0, 0.0)
    for _ in range((TREE - 1).bit_length()):
        half = reach.astype(jnp.bfloat16)
        reach = jnp.minimum(jnp.dot(half, half, preferred_element_type=jnp.float32), 1.0)
    spread = jnp.where(
        lax.broadcasted_iota(i32, (TREE, lanes), 0)
        == lax.broadcasted_iota(i32, (TREE, lanes), 1) % TREE,
        1.0,
        0.0,
    ).astype(jnp.bfloat16)
    linked = jnp.dot(reach.astype(jnp.bfloat16), spread, preferred_element_type=jnp.float32)
    bias[0, pl.ds(positions, TREE), :] = jnp.where(linked > 0.5, 0.0, NEG)

    if span > used:
        kbuf[pl.ds(used, span - used), :] = jnp.zeros((span - used, channels), jnp.bfloat16)
        vbuf[pl.ds(used, span - used), :] = jnp.zeros((span - used, channels), jnp.bfloat16)

    locals_[0].wait()
    locals_[1].wait()
    chosen = jnp.where(
        jnp.broadcast_to(accept_ref[...], (TREE, A_MAX))
        == lax.broadcasted_iota(i32, (TREE, A_MAX), 0),
        1.0,
        0.0,
    ).astype(jnp.bfloat16)
    dims = (((0,), (0,)), ((), ()))
    tree_rows = pl.ds(positions, TREE)
    rows[...] = jnp.concatenate(
        [
            lax.dot_general(chosen, kbuf[tree_rows, :], dims, preferred_element_type=jnp.float32),
            lax.dot_general(chosen, vbuf[tree_rows, :], dims, preferred_element_type=jnp.float32),
        ],
        axis=0,
    ).astype(jnp.bfloat16)
    for d in range(1, GROUP):
        r_copy(d).start()

    for i in (2, 3, 4):
        locals_[i].wait()
    for k in range(kv):
        vt[k] = vbuf[:, k * HD : (k + 1) * HD].astype(jnp.float32).T.astype(jnp.bfloat16)

    def attend(queries, k, which):
        stacked = jnp.concatenate(
            [queries[:, g * HD : (g + 1) * HD] for g in range(sharing)], axis=0
        )
        keys = kbuf[:, pl.ds(pl.multiple_of(k * HD, HD), HD)]
        scores = lax.dot_general(
            keys, stacked, (((1,), (1,)), ((), ())), preferred_element_type=jnp.float32
        )
        scores = scores + bias[which]
        top = jnp.maximum(jnp.max(scores, axis=0, keepdims=True), FLOOR)
        top = top.astype(jnp.bfloat16).astype(jnp.float32)
        raised = jnp.exp2((scores - top) * scale)
        total = jnp.sum(raised, axis=0, keepdims=True)
        out = jnp.dot(vt[k], raised.astype(jnp.bfloat16), preferred_element_type=jnp.float32)
        return out, top, total

    def own_step(k, carry):
        out, top, total = attend(qown[:, pl.ds(pl.multiple_of(k * qk, qk), qk)], k, 0)
        own_o[k] = out
        own_s[k] = jnp.concatenate(
            [top, total, jnp.zeros((6, lanes), jnp.float32)], axis=0
        )
        return carry


    tail_row = lax.broadcasted_iota(i32, (TAIL, lanes), 0)

    def answer(k, ds):
        found = [attend(qbuf[d - 1, k], k, d) for d in ds]
        for d, (out, top, total) in zip(ds, found):
            psend[d - 1, k, pl.ds(0, HD), :] = out.astype(jnp.bfloat16)
            main = total.astype(jnp.bfloat16).astype(jnp.float32)
            tail = jnp.where(
                tail_row == 0, top, jnp.where(tail_row == 1, main, total - main)
            )
            psend[d - 1, k, pl.ds(HD, TAIL), :] = tail.astype(jnp.bfloat16)
        for d in ds:
            p_copy(d, k).start()

    for k in range(kv):
        q_copy(1, k).wait_recv()
        q_copy(2, k).wait_recv()
        forward(k, 1 + k % 2).start()
        answer(k, (1, 2))

    def far_step(k, carry):
        q_copy(3, k).wait_recv()
        answer(k, (3,))
        return carry

    lax.fori_loop(0, kv, far_step, 0)
    lax.fori_loop(0, kv, own_step, 0)

    for d in range(1, GROUP):
        r_copy(d).wait_recv()
    wide = GROUP * 2 * A_MAX
    col = lax.broadcasted_iota(i32, (1, wide), 1)
    slot = col % (2 * A_MAX)
    targets = jnp.full((1, wide), -1, i32)
    for d in range(GROUP):
        peer = peer_of(d)
        end, taken = begins[0] + lens[0], acc_len_ref[base]
        for r in range(1, GROUP):
            end = jnp.where(peer == r, begins[r] + lens[r], end)
            taken = jnp.where(peer == r, acc_len_ref[base + r], taken)
        hit = (col // (2 * A_MAX) == d) & (slot % A_MAX < taken)
        targets = jnp.where(hit, end + slot % A_MAX, targets)
    arrived = jnp.concatenate([rows[...]] + [rrecv[d] for d in range(GROUP - 1)], axis=0)
    where_row = lax.broadcasted_iota(i32, (positions, wide), 0)
    outs = []
    for half, (old, new, dest) in enumerate(((kbuf, nk, nk_hbm), (vbuf, nv, nv_hbm))):
        mine = jnp.where(slot // A_MAX == half, targets, -1)
        pick = jnp.where(where_row == mine, 1.0, 0.0)
        changed = jnp.max(pick, axis=1, keepdims=True)
        put = jnp.dot(pick.astype(jnp.bfloat16), arrived, preferred_element_type=jnp.float32)
        new[...] = jnp.where(changed > 0.5, put, old[pl.ds(0, positions), :].astype(jnp.float32)).astype(
            jnp.bfloat16
        )
        copy = pltpu.make_async_copy(new, dest, out_sem.at[half])
        copy.start()
        outs.append(copy)

    def gather(k):
        tops = [own_s[k, pl.ds(0, 1), :]]
        totals = [own_s[k, pl.ds(1, 1), :]]
        parts = [own_o[k]]
        for d in (1, 2, 3):
            p_copy(d, k).wait_recv()
            tail = precv[d - 1, k, pl.ds(HD, TAIL), :].astype(jnp.float32)
            tops.append(tail[0:1])
            totals.append(tail[1:2] + tail[2:3])
            parts.append(precv[d - 1, k, pl.ds(0, HD), :].astype(jnp.float32))
        top = functools.reduce(jnp.maximum, tops)
        factors = [jnp.exp2((t - top) * scale) for t in tops]
        total = sum(f * t for f, t in zip(factors, totals))
        out = sum(f * p for f, p in zip(factors, parts)) * (1.0 / total)
        turned = out.T.astype(jnp.bfloat16)
        for g in range(sharing):
            att[:, g * HD : (g + 1) * HD] = turned[g * TREE : (g + 1) * TREE]

    step = min(w_loc, 1024)

    def project(k, d):
        peer = (tp + d) % n_tp
        left = att[...]
        for c in range(w_loc // step):
            columns = pl.ds(pl.multiple_of(peer * w_loc + c * step, HD), step)
            part = jnp.dot(
                left,
                wbuf[pl.ds(pl.multiple_of(k * qk, qk), qk), columns],
                preferred_element_type=jnp.float32,
            )
            acc[d, :, c * step : (c + 1) * step] += part

    acc[...] = jnp.zeros_like(acc)

    def out_step(k, carry):
        w_copy(k).wait()
        gather(k)
        for d in range(n_tp):
            project(k, d)
        return carry

    lax.fori_loop(0, kv - 1, out_step, 0)
    w_copy(kv - 1).wait()
    gather(kv - 1)
    for d in range(1, n_tp):
        project(kv - 1, d)
        tsend[d - 1] = acc[d].astype(jnp.bfloat16)
        t_copy(d).start()
    project(kv - 1, 0)
    locals_[5].wait()
    result = acc[0] + resbuf[...].astype(jnp.float32)
    for d in range(1, n_tp):
        t_copy(d).wait_recv()
        result = result + trecv[d - 1].astype(jnp.float32)
    mixed_ref[0] = result.astype(jnp.bfloat16)

    for copy in outs:
        copy.wait()
    for d in range(1, GROUP):
        r_copy(d).wait_send()
        for k in range(kv):
            if d < 3:
                q_copy(d, k).wait_send()
            else:
                forward(k, 1 + k % 2).wait_send()
            p_copy(d, k).wait_send()
    for d in range(1, n_tp):
        t_copy(d).wait_send()


def write_out(a, b, c, a_out, b_out, c_out, a_mem, b_mem, c_mem, in_sem, sem):
    hops = [(a, a_mem, a_out)]
    part = b.shape[0] // CUTS
    for src, mem, dst in ((b, b_mem, b_out), (c, c_mem, c_out)):
        for i in range(CUTS):
            rows = pl.ds(i * part, part)
            hops.append((src.at[rows], mem.at[rows], dst.at[rows]))
    loads = [pltpu.make_async_copy(x, m, in_sem.at[i]) for i, (x, m, y) in enumerate(hops)]
    stores = [pltpu.make_async_copy(m, y, sem.at[i]) for i, (x, m, y) in enumerate(hops)]
    for copy in loads:
        copy.start()
    for load, store in zip(loads, stores):
        load.wait()
        store.start()
    for copy in stores:
        copy.wait()


def on_device(n_tp, queries, tree_keys, tree_values, cache_keys, cache_values, residual, out_weight, cache_len, parents, accept_rows, accept_len):
    positions, channels = cache_keys.shape
    kv = channels // HD
    q_width = queries.shape[2]
    qk = q_width // kv
    lanes = qk // HD * TREE
    w_loc = residual.shape[2]
    span = -(-(positions + TREE) // 128) * 128
    bf16, f32 = jnp.bfloat16, jnp.float32
    peers = GROUP - 1
    vmem = pltpu.VMEM
    dma = pltpu.SemaphoreType.DMA
    hbm = pl.BlockSpec(memory_space=pltpu.HBM)
    local = pl.BlockSpec(memory_space=pltpu.VMEM)
    results = (
        jax.ShapeDtypeStruct(residual.shape, bf16),
        jax.ShapeDtypeStruct(cache_keys.shape, bf16),
        jax.ShapeDtypeStruct(cache_values.shape, bf16),
    )
    made = pl.pallas_call(
        functools.partial(kernel, n_tp),
        out_shape=results,
        in_specs=[hbm] * 11,
        out_specs=(local, hbm, hbm),
        scratch_shapes=[
            pltpu.SMEM(cache_len.shape, jnp.int32),
            pltpu.SMEM(accept_len.shape, jnp.int32),
            vmem(parents.shape, jnp.int32),
            vmem(accept_rows.shape, jnp.int32),
            vmem((span, channels), bf16),
            vmem((span, channels), bf16),
            vmem((kv, HD, span), bf16),
            vmem((TREE, q_width), bf16),
            vmem((peers, kv, TREE, qk), bf16),
            vmem((GROUP, span, lanes), f32),
            vmem((kv, HD, lanes), f32),
            vmem((kv, 8, lanes), f32),
            vmem((peers, kv, HD + TAIL, lanes), bf16),
            vmem((peers, kv, HD + TAIL, lanes), bf16),
            vmem((2 * A_MAX, channels), bf16),
            vmem((peers, 2 * A_MAX, channels), bf16),
            vmem(out_weight.shape, bf16),
            vmem((TREE, qk), bf16),
            vmem((n_tp, TREE, w_loc), f32),
            vmem((max(n_tp - 1, 1), TREE, w_loc), bf16),
            vmem((max(n_tp - 1, 1), TREE, w_loc), bf16),
            vmem((TREE, w_loc), bf16),
            vmem((positions, channels), bf16),
            vmem((positions, channels), bf16),
            dma((10,)),
            dma((kv,)),
            dma((2,)),
            dma((peers, kv)),
            dma((peers, kv)),
            dma((peers, kv)),
            dma((peers, kv)),
            dma((peers,)),
            dma((peers,)),
            dma((max(n_tp - 1, 1),)),
            dma((max(n_tp - 1, 1),)),
        ],
        compiler_params=pltpu.CompilerParams(
            collective_id=0, has_side_effects=True, vmem_limit_bytes=62 * 1024 * 1024
        ),
        name="tree_attention",
    )(cache_len, accept_len, parents, accept_rows, queries, tree_keys, tree_values, cache_keys, cache_values, residual, out_weight)
    return pl.pallas_call(
        write_out,
        out_shape=results,
        in_specs=[hbm] * 3,
        out_specs=(hbm, hbm, hbm),
        scratch_shapes=[
            vmem(residual.shape, bf16),
            vmem(cache_keys.shape, bf16),
            vmem(cache_values.shape, bf16),
            dma((2 * CUTS + 1,)),
            dma((2 * CUTS + 1,)),
        ],
        compiler_params=pltpu.CompilerParams(vmem_limit_bytes=62 * 1024 * 1024),
        name="write_out",
    )(*made)


def solution(mesh):
    return jax.shard_map(
        functools.partial(on_device, mesh.shape["tp"]),
        mesh=mesh,
        in_specs=(
            P("seq", None, "tp"),
            P("seq", None, "tp"),
            P("seq", None, "tp"),
            P("seq", "tp"),
            P("seq", "tp"),
            P("seq", None, "tp"),
            P("tp", None),
            P(),
            P("seq", None),
            P("seq", None),
            P(),
        ),
        out_specs=(P("seq", None, "tp"), P("seq", "tp"), P("seq", "tp")),
        check_vma=False,
    )
```

```python
import functools
import math

import jax
import jax.numpy as jnp
from jax import lax
from jax.experimental import pallas as pl
from jax.experimental.pallas import tpu as pltpu
from jax.sharding import PartitionSpec as P

HD = 128
TREE = 32
A_MAX = 8
GROUP = 4
NEG = -1e30
FLOOR = -1e29
TAIL = 16
CUTS = 3
MESH = pl.DeviceIdType.MESH


def kernel(
    n_tp,
    len_hbm,
    acc_len_hbm,
    parents_hbm,
    accept_hbm,
    q_hbm,
    tk_hbm,
    tv_hbm,
    ck_hbm,
    cv_hbm,
    res_hbm,
    w_hbm,
    mixed_ref,
    nk_hbm,
    nv_hbm,
    len_ref,
    acc_len_ref,
    parents_ref,
    accept_ref,
    kbuf,
    vbuf,
    vt,
    qown,
    qbuf,
    bias,
    own_o,
    own_s,
    psend,
    precv,
    rows,
    rrecv,
    wbuf,
    att,
    acc,
    tsend,
    trecv,
    resbuf,
    nk,
    nv,
    loc_sem,
    w_sem,
    out_sem,
    q_ss,
    q_rs,
    p_ss,
    p_rs,
    r_ss,
    r_rs,
    t_ss,
    t_rs,
):
    positions, channels = ck_hbm.shape
    kv = channels // HD
    qk = q_hbm.shape[2] // kv
    sharing = qk // HD
    lanes = sharing * TREE
    span = kbuf.shape[0]
    used = positions + TREE
    w_loc = res_hbm.shape[2]
    scale = math.log2(math.e) / math.sqrt(HD)

    seq = lax.axis_index("seq")
    tp = lax.axis_index("tp")
    base = seq // GROUP * GROUP
    within = seq - base
    low, high = within % 2, within // 2

    def peer_of(d):
        return (low + d % 2) % 2 + 2 * ((high + d // 2) % 2)

    barrier = pltpu.get_barrier_semaphore()
    for d in range(1, GROUP):
        pl.semaphore_signal(barrier, inc=1, device_id=(base + peer_of(d), tp), device_id_type=MESH)
    for d in range(1, n_tp):
        pl.semaphore_signal(barrier, inc=1, device_id=(seq, (tp + d) % n_tp), device_id_type=MESH)
    locals_ = [
        pltpu.make_async_copy(tk_hbm.at[0], kbuf.at[pl.ds(positions, TREE)], loc_sem.at[0]),
        pltpu.make_async_copy(tv_hbm.at[0], vbuf.at[pl.ds(positions, TREE)], loc_sem.at[1]),
        pltpu.make_async_copy(q_hbm.at[0], qown, loc_sem.at[2]),
        pltpu.make_async_copy(ck_hbm, kbuf.at[pl.ds(0, positions)], loc_sem.at[3]),
        pltpu.make_async_copy(cv_hbm, vbuf.at[pl.ds(0, positions)], loc_sem.at[4]),
        pltpu.make_async_copy(res_hbm.at[0], resbuf, loc_sem.at[5]),
        pltpu.make_async_copy(len_hbm, len_ref, loc_sem.at[6]),
        pltpu.make_async_copy(acc_len_hbm, acc_len_ref, loc_sem.at[7]),
        pltpu.make_async_copy(parents_hbm, parents_ref, loc_sem.at[8]),
        pltpu.make_async_copy(accept_hbm, accept_ref, loc_sem.at[9]),
    ]
    for c in locals_:
        c.start()

    pl.semaphore_wait(barrier, GROUP - 1 + n_tp - 1)

    def q_copy(d, k):
        return pltpu.make_async_remote_copy(
            src_ref=q_hbm.at[0, :, pl.ds(pl.multiple_of(k * qk, qk), qk)],
            dst_ref=qbuf.at[d - 1, k],
            send_sem=q_ss.at[d - 1, k],
            recv_sem=q_rs.at[d - 1, k],
            device_id=(base + peer_of(d), tp),
            device_id_type=MESH,
        )

    def p_copy(d, k):
        return pltpu.make_async_remote_copy(
            src_ref=psend.at[d - 1, k],
            dst_ref=precv.at[d - 1, k],
            send_sem=p_ss.at[d - 1, k],
            recv_sem=p_rs.at[d - 1, k],
            device_id=(base + peer_of(d), tp),
            device_id_type=MESH,
        )

    def r_copy(d):
        return pltpu.make_async_remote_copy(
            src_ref=rows,
            dst_ref=rrecv.at[d - 1],
            send_sem=r_ss.at[d - 1],
            recv_sem=r_rs.at[d - 1],
            device_id=(base + peer_of(d), tp),
            device_id_type=MESH,
        )

    def t_copy(d):
        return pltpu.make_async_remote_copy(
            src_ref=tsend.at[d - 1],
            dst_ref=trecv.at[d - 1],
            send_sem=t_ss.at[d - 1],
            recv_sem=t_rs.at[d - 1],
            device_id=(seq, (tp + d) % n_tp),
            device_id_type=MESH,
        )

    def w_copy(k):
        rows_k = pl.ds(pl.multiple_of(k * qk, qk), qk)
        return pltpu.make_async_copy(w_hbm.at[rows_k], wbuf.at[rows_k], w_sem.at[k])

    for k in range(kv):
        for d in (3, 1, 2):
            q_copy(d, k).start()
    for k in range(kv):
        w_copy(k).start()

    for i in (6, 7, 8, 9):
        locals_[i].wait()

    lens = [len_ref[base + r] for r in range(GROUP)]
    begins = []
    at = -within * positions
    for r in range(GROUP):
        begins.append(at)
        at = at + lens[r] + A_MAX
    place = lax.broadcasted_iota(jnp.int32, (positions, lanes), 0)
    for d in range(GROUP):
        peer = peer_of(d)
        first, size = begins[0], lens[0]
        for r in range(1, GROUP):
            first = jnp.where(peer == r, begins[r], first)
            size = jnp.where(peer == r, lens[r], size)
        inside = (place >= first) & (place < first + size)
        bias[pl.ds(0, positions), d * lanes : (d + 1) * lanes] = jnp.where(inside, 0.0, NEG)
        bias[pl.ds(positions, span - positions), d * lanes : (d + 1) * lanes] = jnp.full(
            (span - positions, lanes), NEG, jnp.float32
        )

    i32 = jnp.int32
    row_i = lax.broadcasted_iota(i32, (TREE, TREE), 0)
    col_i = lax.broadcasted_iota(i32, (TREE, TREE), 1)
    parents = jnp.broadcast_to(parents_ref[...], (TREE, TREE))
    reach = jnp.where((row_i == col_i) | (parents == row_i), 1.0, 0.0)
    for _ in range((TREE - 1).bit_length()):
        half = reach.astype(jnp.bfloat16)
        reach = jnp.minimum(jnp.dot(half, half, preferred_element_type=jnp.float32), 1.0)
    spread = jnp.where(
        lax.broadcasted_iota(i32, (TREE, lanes), 0)
        == lax.broadcasted_iota(i32, (TREE, lanes), 1) % TREE,
        1.0,
        0.0,
    ).astype(jnp.bfloat16)
    linked = jnp.dot(reach.astype(jnp.bfloat16), spread, preferred_element_type=jnp.float32)
    bias[pl.ds(positions, TREE), 0:lanes] = jnp.where(linked > 0.5, 0.0, NEG)

    if span > used:
        kbuf[pl.ds(used, span - used), :] = jnp.zeros((span - used, channels), jnp.bfloat16)
        vbuf[pl.ds(used, span - used), :] = jnp.zeros((span - used, channels), jnp.bfloat16)

    locals_[0].wait()
    locals_[1].wait()
    chosen = jnp.where(
        jnp.broadcast_to(accept_ref[...], (TREE, A_MAX))
        == lax.broadcasted_iota(i32, (TREE, A_MAX), 0),
        1.0,
        0.0,
    ).astype(jnp.bfloat16)
    dims = (((0,), (0,)), ((), ()))
    tree_rows = pl.ds(positions, TREE)
    rows[...] = jnp.concatenate(
        [
            lax.dot_general(chosen, kbuf[tree_rows, :], dims, preferred_element_type=jnp.float32),
            lax.dot_general(chosen, vbuf[tree_rows, :], dims, preferred_element_type=jnp.float32),
        ],
        axis=0,
    ).astype(jnp.bfloat16)
    for d in range(1, GROUP):
        r_copy(d).start()

    for i in (2, 3, 4):
        locals_[i].wait()
    for k in range(kv):
        vt[k] = vbuf[:, k * HD : (k + 1) * HD].astype(jnp.float32).T.astype(jnp.bfloat16)

    tail_row = lax.broadcasted_iota(i32, (TAIL, lanes), 0)

    def attend(k, carry):
        for d in (1, 2, 3):
            q_copy(d, k).wait_recv()
        blocks = [qown[:, pl.ds(pl.multiple_of(k * qk, qk), qk)]]
        blocks += [qbuf[d - 1, k] for d in (1, 2, 3)]
        stacked = jnp.concatenate(
            [q[:, g * HD : (g + 1) * HD] for q in blocks for g in range(sharing)], axis=0
        )
        keys = kbuf[:, pl.ds(pl.multiple_of(k * HD, HD), HD)]
        scores = lax.dot_general(
            keys, stacked, (((1,), (1,)), ((), ())), preferred_element_type=jnp.float32
        )
        scores = scores + bias[...]
        top = jnp.maximum(jnp.max(scores, axis=0, keepdims=True), FLOOR)
        top = top.astype(jnp.bfloat16).astype(jnp.float32)
        raised = jnp.exp2((scores - top) * scale)
        total = jnp.sum(raised, axis=0, keepdims=True)
        out = jnp.dot(vt[k], raised.astype(jnp.bfloat16), preferred_element_type=jnp.float32)
        for d in (3, 1, 2):
            mine = slice(d * lanes, (d + 1) * lanes)
            psend[d - 1, k, pl.ds(0, HD), :] = out[:, mine].astype(jnp.bfloat16)
            whole = total[:, mine]
            main = whole.astype(jnp.bfloat16).astype(jnp.float32)
            tail = jnp.where(
                tail_row == 0, top[:, mine], jnp.where(tail_row == 1, main, whole - main)
            )
            psend[d - 1, k, pl.ds(HD, TAIL), :] = tail.astype(jnp.bfloat16)
        for d in (3, 1, 2):
            p_copy(d, k).start()
        own_o[k] = out[:, :lanes]
        own_s[k] = jnp.concatenate(
            [top[:, :lanes], total[:, :lanes], jnp.zeros((6, lanes), jnp.float32)], axis=0
        )
        return carry

    lax.fori_loop(0, kv, attend, 0)

    for d in range(1, GROUP):
        r_copy(d).wait_recv()
    wide = GROUP * 2 * A_MAX
    col = lax.broadcasted_iota(i32, (1, wide), 1)
    slot = col % (2 * A_MAX)
    targets = jnp.full((1, wide), -1, i32)
    for d in range(GROUP):
        peer = peer_of(d)
        end, taken = begins[0] + lens[0], acc_len_ref[base]
        for r in range(1, GROUP):
            end = jnp.where(peer == r, begins[r] + lens[r], end)
            taken = jnp.where(peer == r, acc_len_ref[base + r], taken)
        hit = (col // (2 * A_MAX) == d) & (slot % A_MAX < taken)
        targets = jnp.where(hit, end + slot % A_MAX, targets)
    arrived = jnp.concatenate([rows[...]] + [rrecv[d] for d in range(GROUP - 1)], axis=0)
    where_row = lax.broadcasted_iota(i32, (positions, wide), 0)
    outs = []
    for half, (old, new, dest) in enumerate(((kbuf, nk, nk_hbm), (vbuf, nv, nv_hbm))):
        mine = jnp.where(slot // A_MAX == half, targets, -1)
        pick = jnp.where(where_row == mine, 1.0, 0.0)
        changed = jnp.max(pick, axis=1, keepdims=True)
        put = jnp.dot(pick.astype(jnp.bfloat16), arrived, preferred_element_type=jnp.float32)
        new[...] = jnp.where(changed > 0.5, put, old[pl.ds(0, positions), :].astype(jnp.float32)).astype(
            jnp.bfloat16
        )
        copy = pltpu.make_async_copy(new, dest, out_sem.at[half])
        copy.start()
        outs.append(copy)

    def gather(k):
        tops = [own_s[k, pl.ds(0, 1), :]]
        totals = [own_s[k, pl.ds(1, 1), :]]
        parts = [own_o[k]]
        for d in (1, 2, 3):
            p_copy(d, k).wait_recv()
            tail = precv[d - 1, k, pl.ds(HD, TAIL), :].astype(jnp.float32)
            tops.append(tail[0:1])
            totals.append(tail[1:2] + tail[2:3])
            parts.append(precv[d - 1, k, pl.ds(0, HD), :].astype(jnp.float32))
        top = functools.reduce(jnp.maximum, tops)
        factors = [jnp.exp2((t - top) * scale) for t in tops]
        total = sum(f * t for f, t in zip(factors, totals))
        out = sum(f * p for f, p in zip(factors, parts)) * (1.0 / total)
        turned = out.T.astype(jnp.bfloat16)
        for g in range(sharing):
            att[:, g * HD : (g + 1) * HD] = turned[g * TREE : (g + 1) * TREE]

    step = min(w_loc, 1024)

    def project(k, d):
        peer = (tp + d) % n_tp
        left = att[...]
        for c in range(w_loc // step):
            columns = pl.ds(pl.multiple_of(peer * w_loc + c * step, HD), step)
            part = jnp.dot(
                left,
                wbuf[pl.ds(pl.multiple_of(k * qk, qk), qk), columns],
                preferred_element_type=jnp.float32,
            )
            acc[d, :, c * step : (c + 1) * step] += part

    acc[...] = jnp.zeros_like(acc)

    def out_step(k, carry):
        w_copy(k).wait()
        gather(k)
        for d in range(n_tp):
            project(k, d)
        return carry

    lax.fori_loop(0, kv - 1, out_step, 0)
    w_copy(kv - 1).wait()
    gather(kv - 1)
    for d in range(1, n_tp):
        project(kv - 1, d)
        tsend[d - 1] = acc[d].astype(jnp.bfloat16)
        t_copy(d).start()
    project(kv - 1, 0)
    locals_[5].wait()
    result = acc[0] + resbuf[...].astype(jnp.float32)
    for d in range(1, n_tp):
        t_copy(d).wait_recv()
        result = result + trecv[d - 1].astype(jnp.float32)
    mixed_ref[0] = result.astype(jnp.bfloat16)

    for copy in outs:
        copy.wait()
    for d in range(1, GROUP):
        r_copy(d).wait_send()
        for k in range(kv):
            q_copy(d, k).wait_send()
            p_copy(d, k).wait_send()
    for d in range(1, n_tp):
        t_copy(d).wait_send()


def write_out(a, b, c, a_out, b_out, c_out, a_mem, b_mem, c_mem, in_sem, sem):
    hops = [(a, a_mem, a_out)]
    part = b.shape[0] // CUTS
    for src, mem, dst in ((b, b_mem, b_out), (c, c_mem, c_out)):
        for i in range(CUTS):
            rows = pl.ds(i * part, part)
            hops.append((src.at[rows], mem.at[rows], dst.at[rows]))
    loads = [pltpu.make_async_copy(x, m, in_sem.at[i]) for i, (x, m, y) in enumerate(hops)]
    stores = [pltpu.make_async_copy(m, y, sem.at[i]) for i, (x, m, y) in enumerate(hops)]
    for copy in loads:
        copy.start()
    for load, store in zip(loads, stores):
        load.wait()
        store.start()
    for copy in stores:
        copy.wait()


def on_device(n_tp, queries, tree_keys, tree_values, cache_keys, cache_values, residual, out_weight, cache_len, parents, accept_rows, accept_len):
    positions, channels = cache_keys.shape
    kv = channels // HD
    q_width = queries.shape[2]
    qk = q_width // kv
    lanes = qk // HD * TREE
    w_loc = residual.shape[2]
    span = -(-(positions + TREE) // 128) * 128
    bf16, f32 = jnp.bfloat16, jnp.float32
    peers = GROUP - 1
    vmem = pltpu.VMEM
    dma = pltpu.SemaphoreType.DMA
    hbm = pl.BlockSpec(memory_space=pltpu.HBM)
    local = pl.BlockSpec(memory_space=pltpu.VMEM)
    results = (
        jax.ShapeDtypeStruct(residual.shape, bf16),
        jax.ShapeDtypeStruct(cache_keys.shape, bf16),
        jax.ShapeDtypeStruct(cache_values.shape, bf16),
    )
    made = pl.pallas_call(
        functools.partial(kernel, n_tp),
        out_shape=results,
        in_specs=[hbm] * 11,
        out_specs=(local, hbm, hbm),
        scratch_shapes=[
            pltpu.SMEM(cache_len.shape, jnp.int32),
            pltpu.SMEM(accept_len.shape, jnp.int32),
            vmem(parents.shape, jnp.int32),
            vmem(accept_rows.shape, jnp.int32),
            vmem((span, channels), bf16),
            vmem((span, channels), bf16),
            vmem((kv, HD, span), bf16),
            vmem((TREE, q_width), bf16),
            vmem((peers, kv, TREE, qk), bf16),
            vmem((span, GROUP * lanes), f32),
            vmem((kv, HD, lanes), f32),
            vmem((kv, 8, lanes), f32),
            vmem((peers, kv, HD + TAIL, lanes), bf16),
            vmem((peers, kv, HD + TAIL, lanes), bf16),
            vmem((2 * A_MAX, channels), bf16),
            vmem((peers, 2 * A_MAX, channels), bf16),
            vmem(out_weight.shape, bf16),
            vmem((TREE, qk), bf16),
            vmem((n_tp, TREE, w_loc), f32),
            vmem((max(n_tp - 1, 1), TREE, w_loc), bf16),
            vmem((max(n_tp - 1, 1), TREE, w_loc), bf16),
            vmem((TREE, w_loc), bf16),
            vmem((positions, channels), bf16),
            vmem((positions, channels), bf16),
            dma((10,)),
            dma((kv,)),
            dma((2,)),
            dma((peers, kv)),
            dma((peers, kv)),
            dma((peers, kv)),
            dma((peers, kv)),
            dma((peers,)),
            dma((peers,)),
            dma((max(n_tp - 1, 1),)),
            dma((max(n_tp - 1, 1),)),
        ],
        compiler_params=pltpu.CompilerParams(
            collective_id=0, has_side_effects=True, vmem_limit_bytes=62 * 1024 * 1024
        ),
        name="tree_attention",
    )(cache_len, accept_len, parents, accept_rows, queries, tree_keys, tree_values, cache_keys, cache_values, residual, out_weight)
    return pl.pallas_call(
        write_out,
        out_shape=results,
        in_specs=[hbm] * 3,
        out_specs=(hbm, hbm, hbm),
        scratch_shapes=[
            vmem(residual.shape, bf16),
            vmem(cache_keys.shape, bf16),
            vmem(cache_values.shape, bf16),
            dma((2 * CUTS + 1,)),
            dma((2 * CUTS + 1,)),
        ],
        compiler_params=pltpu.CompilerParams(vmem_limit_bytes=62 * 1024 * 1024),
        name="write_out",
    )(*made)


def solution(mesh):
    return jax.shard_map(
        functools.partial(on_device, mesh.shape["tp"]),
        mesh=mesh,
        in_specs=(
            P("seq", None, "tp"),
            P("seq", None, "tp"),
            P("seq", None, "tp"),
            P("seq", "tp"),
            P("seq", "tp"),
            P("seq", None, "tp"),
            P("tp", None),
            P(),
            P("seq", None),
            P("seq", None),
            P(),
        ),
        out_specs=(P("seq", None, "tp"), P("seq", "tp"), P("seq", "tp")),
        check_vma=False,
    )
```

```python
import functools
import math

import jax
import jax.numpy as jnp
from jax import lax
from jax.experimental import pallas as pl
from jax.experimental.pallas import tpu as pltpu
from jax.sharding import PartitionSpec as P

HD = 128
TREE = 32
A_MAX = 8
GROUP = 4
NEG = -1e30
FLOOR = -1e29
TAIL = 16
CUTS = 3
MESH = pl.DeviceIdType.MESH


def kernel(
    n_tp,
    len_hbm,
    acc_len_hbm,
    parents_hbm,
    accept_hbm,
    q_hbm,
    tk_hbm,
    tv_hbm,
    ck_hbm,
    cv_hbm,
    res_hbm,
    w_hbm,
    mixed_ref,
    nk_hbm,
    nv_hbm,
    len_ref,
    acc_len_ref,
    parents_ref,
    accept_ref,
    kbuf,
    vbuf,
    vt,
    qown,
    qbuf,
    bias,
    own_o,
    own_s,
    psend,
    precv,
    rows,
    rrecv,
    wbuf,
    att,
    acc,
    tsend,
    trecv,
    resbuf,
    nk,
    nv,
    loc_sem,
    w_sem,
    out_sem,
    q_ss,
    q_rs,
    p_ss,
    p_rs,
    r_ss,
    r_rs,
    t_ss,
    t_rs,
):
    positions, channels = ck_hbm.shape
    kv = channels // HD
    qk = q_hbm.shape[2] // kv
    sharing = qk // HD
    lanes = sharing * TREE
    span = kbuf.shape[0]
    used = positions + TREE
    w_loc = res_hbm.shape[2]
    scale = math.log2(math.e) / math.sqrt(HD)

    seq = lax.axis_index("seq")
    tp = lax.axis_index("tp")
    base = seq // GROUP * GROUP
    within = seq - base
    low, high = within % 2, within // 2

    def peer_of(d):
        return (low + d % 2) % 2 + 2 * ((high + d // 2) % 2)

    barrier = pltpu.get_barrier_semaphore()
    for d in range(1, GROUP):
        pl.semaphore_signal(barrier, inc=1, device_id=(base + peer_of(d), tp), device_id_type=MESH)
    for d in range(1, n_tp):
        pl.semaphore_signal(barrier, inc=1, device_id=(seq, (tp + d) % n_tp), device_id_type=MESH)
    locals_ = [
        pltpu.make_async_copy(tk_hbm.at[0], kbuf.at[pl.ds(positions, TREE)], loc_sem.at[0]),
        pltpu.make_async_copy(tv_hbm.at[0], vbuf.at[pl.ds(positions, TREE)], loc_sem.at[1]),
        pltpu.make_async_copy(q_hbm.at[0], qown, loc_sem.at[2]),
        pltpu.make_async_copy(ck_hbm, kbuf.at[pl.ds(0, positions)], loc_sem.at[3]),
        pltpu.make_async_copy(cv_hbm, vbuf.at[pl.ds(0, positions)], loc_sem.at[4]),
        pltpu.make_async_copy(res_hbm.at[0], resbuf, loc_sem.at[5]),
        pltpu.make_async_copy(len_hbm, len_ref, loc_sem.at[6]),
        pltpu.make_async_copy(acc_len_hbm, acc_len_ref, loc_sem.at[7]),
        pltpu.make_async_copy(parents_hbm, parents_ref, loc_sem.at[8]),
        pltpu.make_async_copy(accept_hbm, accept_ref, loc_sem.at[9]),
    ]
    for c in locals_:
        c.start()

    pl.semaphore_wait(barrier, GROUP - 1 + n_tp - 1)

    def q_copy(d, k):
        return pltpu.make_async_remote_copy(
            src_ref=q_hbm.at[0, :, pl.ds(pl.multiple_of(k * qk, qk), qk)],
            dst_ref=qbuf.at[d - 1, k],
            send_sem=q_ss.at[d - 1, k],
            recv_sem=q_rs.at[d - 1, k],
            device_id=(base + peer_of(d), tp),
            device_id_type=MESH,
        )

    def p_copy(d, k):
        return pltpu.make_async_remote_copy(
            src_ref=psend.at[d - 1, k],
            dst_ref=precv.at[d - 1, k],
            send_sem=p_ss.at[d - 1, k],
            recv_sem=p_rs.at[d - 1, k],
            device_id=(base + peer_of(d), tp),
            device_id_type=MESH,
        )

    def r_copy(d):
        return pltpu.make_async_remote_copy(
            src_ref=rows,
            dst_ref=rrecv.at[d - 1],
            send_sem=r_ss.at[d - 1],
            recv_sem=r_rs.at[d - 1],
            device_id=(base + peer_of(d), tp),
            device_id_type=MESH,
        )

    def t_copy(d):
        return pltpu.make_async_remote_copy(
            src_ref=tsend.at[d - 1],
            dst_ref=trecv.at[d - 1],
            send_sem=t_ss.at[d - 1],
            recv_sem=t_rs.at[d - 1],
            device_id=(seq, (tp + d) % n_tp),
            device_id_type=MESH,
        )

    def w_copy(k):
        rows_k = pl.ds(pl.multiple_of(k * qk, qk), qk)
        return pltpu.make_async_copy(w_hbm.at[rows_k], wbuf.at[rows_k], w_sem.at[k])

    for k in range(kv):
        for d in (3, 1, 2):
            q_copy(d, k).start()
    for k in range(kv):
        w_copy(k).start()

    for i in (6, 7, 8, 9):
        locals_[i].wait()

    lens = [len_ref[base + r] for r in range(GROUP)]
    begins = []
    at = -within * positions
    for r in range(GROUP):
        begins.append(at)
        at = at + lens[r] + A_MAX
    place = lax.broadcasted_iota(jnp.int32, (positions, lanes), 0)
    for d in range(GROUP):
        peer = peer_of(d)
        first, size = begins[0], lens[0]
        for r in range(1, GROUP):
            first = jnp.where(peer == r, begins[r], first)
            size = jnp.where(peer == r, lens[r], size)
        inside = (place >= first) & (place < first + size)
        bias[pl.ds(0, positions), d * lanes : (d + 1) * lanes] = jnp.where(inside, 0.0, NEG)
        bias[pl.ds(positions, span - positions), d * lanes : (d + 1) * lanes] = jnp.full(
            (span - positions, lanes), NEG, jnp.float32
        )

    i32 = jnp.int32
    row_i = lax.broadcasted_iota(i32, (TREE, TREE), 0)
    col_i = lax.broadcasted_iota(i32, (TREE, TREE), 1)
    parents = jnp.broadcast_to(parents_ref[...], (TREE, TREE))
    reach = jnp.where((row_i == col_i) | (parents == row_i), 1.0, 0.0)
    for _ in range((TREE - 1).bit_length()):
        half = reach.astype(jnp.bfloat16)
        reach = jnp.minimum(jnp.dot(half, half, preferred_element_type=jnp.float32), 1.0)
    spread = jnp.where(
        lax.broadcasted_iota(i32, (TREE, lanes), 0)
        == lax.broadcasted_iota(i32, (TREE, lanes), 1) % TREE,
        1.0,
        0.0,
    ).astype(jnp.bfloat16)
    linked = jnp.dot(reach.astype(jnp.bfloat16), spread, preferred_element_type=jnp.float32)
    bias[pl.ds(positions, TREE), 0:lanes] = jnp.where(linked > 0.5, 0.0, NEG)

    if span > used:
        kbuf[pl.ds(used, span - used), :] = jnp.zeros((span - used, channels), jnp.bfloat16)
        vbuf[pl.ds(used, span - used), :] = jnp.zeros((span - used, channels), jnp.bfloat16)

    locals_[0].wait()
    locals_[1].wait()
    chosen = jnp.where(
        jnp.broadcast_to(accept_ref[...], (TREE, A_MAX))
        == lax.broadcasted_iota(i32, (TREE, A_MAX), 0),
        1.0,
        0.0,
    ).astype(jnp.bfloat16)
    dims = (((0,), (0,)), ((), ()))
    tree_rows = pl.ds(positions, TREE)
    rows[...] = jnp.concatenate(
        [
            lax.dot_general(chosen, kbuf[tree_rows, :], dims, preferred_element_type=jnp.float32),
            lax.dot_general(chosen, vbuf[tree_rows, :], dims, preferred_element_type=jnp.float32),
        ],
        axis=0,
    ).astype(jnp.bfloat16)
    for d in range(1, GROUP):
        r_copy(d).start()

    for i in (2, 3, 4):
        locals_[i].wait()
    for k in range(kv):
        vt[k] = vbuf[:, k * HD : (k + 1) * HD].astype(jnp.float32).T.astype(jnp.bfloat16)

    tail_row = lax.broadcasted_iota(i32, (TAIL, lanes), 0)

    def attend(k, carry):
        for d in (1, 2, 3):
            q_copy(d, k).wait_recv()
        blocks = [qown[:, pl.ds(pl.multiple_of(k * qk, qk), qk)]]
        blocks += [qbuf[d - 1, k] for d in (1, 2, 3)]
        stacked = jnp.concatenate(
            [q[:, g * HD : (g + 1) * HD] for q in blocks for g in range(sharing)], axis=0
        )
        keys = kbuf[:, pl.ds(pl.multiple_of(k * HD, HD), HD)]
        scores = lax.dot_general(
            keys, stacked, (((1,), (1,)), ((), ())), preferred_element_type=jnp.float32
        )
        scores = scores + bias[...]
        top = jnp.maximum(jnp.max(scores, axis=0, keepdims=True), FLOOR)
        top = top.astype(jnp.bfloat16).astype(jnp.float32)
        raised = jnp.exp2((scores - top) * scale)
        total = jnp.sum(raised, axis=0, keepdims=True)
        out = jnp.dot(vt[k], raised.astype(jnp.bfloat16), preferred_element_type=jnp.float32)
        for d in (3, 1, 2):
            mine = slice(d * lanes, (d + 1) * lanes)
            psend[d - 1, k, pl.ds(0, HD), :] = out[:, mine].astype(jnp.bfloat16)
            whole = total[:, mine]
            main = whole.astype(jnp.bfloat16).astype(jnp.float32)
            tail = jnp.where(
                tail_row == 0, top[:, mine], jnp.where(tail_row == 1, main, whole - main)
            )
            psend[d - 1, k, pl.ds(HD, TAIL), :] = tail.astype(jnp.bfloat16)
        for d in (3, 1, 2):
            p_copy(d, k).start()
        own_o[k] = out[:, :lanes]
        own_s[k] = jnp.concatenate(
            [top[:, :lanes], total[:, :lanes], jnp.zeros((6, lanes), jnp.float32)], axis=0
        )
        return carry

    lax.fori_loop(0, kv, attend, 0)

    for d in range(1, GROUP):
        r_copy(d).wait_recv()
    wide = GROUP * 2 * A_MAX
    col = lax.broadcasted_iota(i32, (1, wide), 1)
    slot = col % (2 * A_MAX)
    targets = jnp.full((1, wide), -1, i32)
    for d in range(GROUP):
        peer = peer_of(d)
        end, taken = begins[0] + lens[0], acc_len_ref[base]
        for r in range(1, GROUP):
            end = jnp.where(peer == r, begins[r] + lens[r], end)
            taken = jnp.where(peer == r, acc_len_ref[base + r], taken)
        hit = (col // (2 * A_MAX) == d) & (slot % A_MAX < taken)
        targets = jnp.where(hit, end + slot % A_MAX, targets)
    arrived = jnp.concatenate([rows[...]] + [rrecv[d] for d in range(GROUP - 1)], axis=0)
    where_row = lax.broadcasted_iota(i32, (positions, wide), 0)
    outs = []
    for half, (old, new, dest) in enumerate(((kbuf, nk, nk_hbm), (vbuf, nv, nv_hbm))):
        mine = jnp.where(slot // A_MAX == half, targets, -1)
        pick = jnp.where(where_row == mine, 1.0, 0.0)
        changed = jnp.max(pick, axis=1, keepdims=True)
        put = jnp.dot(pick.astype(jnp.bfloat16), arrived, preferred_element_type=jnp.float32)
        new[...] = jnp.where(changed > 0.5, put, old[pl.ds(0, positions), :].astype(jnp.float32)).astype(
            jnp.bfloat16
        )
        copy = pltpu.make_async_copy(new, dest, out_sem.at[half])
        copy.start()
        outs.append(copy)

    def gather(k):
        tops = [own_s[k, pl.ds(0, 1), :]]
        totals = [own_s[k, pl.ds(1, 1), :]]
        parts = [own_o[k]]
        for d in (1, 2, 3):
            p_copy(d, k).wait_recv()
            tail = precv[d - 1, k, pl.ds(HD, TAIL), :].astype(jnp.float32)
            tops.append(tail[0:1])
            totals.append(tail[1:2] + tail[2:3])
            parts.append(precv[d - 1, k, pl.ds(0, HD), :].astype(jnp.float32))
        top = functools.reduce(jnp.maximum, tops)
        factors = [jnp.exp2((t - top) * scale) for t in tops]
        total = sum(f * t for f, t in zip(factors, totals))
        out = sum(f * p for f, p in zip(factors, parts)) * (1.0 / total)
        turned = out.T.astype(jnp.bfloat16)
        for g in range(sharing):
            att[:, g * HD : (g + 1) * HD] = turned[g * TREE : (g + 1) * TREE]

    step = min(w_loc, 1024)

    def project(k, d):
        peer = (tp + d) % n_tp
        left = att[...]
        for c in range(w_loc // step):
            columns = pl.ds(pl.multiple_of(peer * w_loc + c * step, HD), step)
            part = jnp.dot(
                left,
                wbuf[pl.ds(pl.multiple_of(k * qk, qk), qk), columns],
                preferred_element_type=jnp.float32,
            )
            acc[d, :, c * step : (c + 1) * step] += part

    acc[...] = jnp.zeros_like(acc)

    def out_step(k, carry):
        w_copy(k).wait()
        gather(k)
        for d in range(n_tp):
            project(k, d)
        return carry

    lax.fori_loop(0, kv - 1, out_step, 0)
    w_copy(kv - 1).wait()
    gather(kv - 1)
    for d in range(1, n_tp):
        project(kv - 1, d)
        tsend[d - 1] = acc[d].astype(jnp.bfloat16)
        t_copy(d).start()
    project(kv - 1, 0)
    locals_[5].wait()
    result = acc[0] + resbuf[...].astype(jnp.float32)
    for d in range(1, n_tp):
        t_copy(d).wait_recv()
        result = result + trecv[d - 1].astype(jnp.float32)
    mixed_ref[0] = result.astype(jnp.bfloat16)

    for copy in outs:
        copy.wait()
    for d in range(1, GROUP):
        r_copy(d).wait_send()
        for k in range(kv):
            q_copy(d, k).wait_send()
            p_copy(d, k).wait_send()
    for d in range(1, n_tp):
        t_copy(d).wait_send()


def write_out(a, b, c, a_out, b_out, c_out, a_mem, b_mem, c_mem, in_sem, sem):
    hops = [(a, a_mem, a_out)]
    part = b.shape[0] // CUTS
    for src, mem, dst in ((b, b_mem, b_out), (c, c_mem, c_out)):
        for i in range(CUTS):
            rows = pl.ds(i * part, part)
            hops.append((src.at[rows], mem.at[rows], dst.at[rows]))
    loads = [pltpu.make_async_copy(x, m, in_sem.at[i]) for i, (x, m, y) in enumerate(hops)]
    stores = [pltpu.make_async_copy(m, y, sem.at[i]) for i, (x, m, y) in enumerate(hops)]
    for copy in loads:
        copy.start()
    for load, store in zip(loads, stores):
        load.wait()
        store.start()
    for copy in stores:
        copy.wait()


def on_device(n_tp, queries, tree_keys, tree_values, cache_keys, cache_values, residual, out_weight, cache_len, parents, accept_rows, accept_len):
    positions, channels = cache_keys.shape
    kv = channels // HD
    q_width = queries.shape[2]
    qk = q_width // kv
    lanes = qk // HD * TREE
    w_loc = residual.shape[2]
    span = positions + TREE
    bf16, f32 = jnp.bfloat16, jnp.float32
    peers = GROUP - 1
    vmem = pltpu.VMEM
    dma = pltpu.SemaphoreType.DMA
    hbm = pl.BlockSpec(memory_space=pltpu.HBM)
    local = pl.BlockSpec(memory_space=pltpu.VMEM)
    results = (
        jax.ShapeDtypeStruct(residual.shape, bf16),
        jax.ShapeDtypeStruct(cache_keys.shape, bf16),
        jax.ShapeDtypeStruct(cache_values.shape, bf16),
    )
    made = pl.pallas_call(
        functools.partial(kernel, n_tp),
        out_shape=results,
        in_specs=[hbm] * 11,
        out_specs=(local, hbm, hbm),
        scratch_shapes=[
            pltpu.SMEM(cache_len.shape, jnp.int32),
            pltpu.SMEM(accept_len.shape, jnp.int32),
            vmem(parents.shape, jnp.int32),
            vmem(accept_rows.shape, jnp.int32),
            vmem((span, channels), bf16),
            vmem((span, channels), bf16),
            vmem((kv, HD, span), bf16),
            vmem((TREE, q_width), bf16),
            vmem((peers, kv, TREE, qk), bf16),
            vmem((span, GROUP * lanes), f32),
            vmem((kv, HD, lanes), f32),
            vmem((kv, 8, lanes), f32),
            vmem((peers, kv, HD + TAIL, lanes), bf16),
            vmem((peers, kv, HD + TAIL, lanes), bf16),
            vmem((2 * A_MAX, channels), bf16),
            vmem((peers, 2 * A_MAX, channels), bf16),
            vmem(out_weight.shape, bf16),
            vmem((TREE, qk), bf16),
            vmem((n_tp, TREE, w_loc), f32),
            vmem((max(n_tp - 1, 1), TREE, w_loc), bf16),
            vmem((max(n_tp - 1, 1), TREE, w_loc), bf16),
            vmem((TREE, w_loc), bf16),
            vmem((positions, channels), bf16),
            vmem((positions, channels), bf16),
            dma((10,)),
            dma((kv,)),
            dma((2,)),
            dma((peers, kv)),
            dma((peers, kv)),
            dma((peers, kv)),
            dma((peers, kv)),
            dma((peers,)),
            dma((peers,)),
            dma((max(n_tp - 1, 1),)),
            dma((max(n_tp - 1, 1),)),
        ],
        compiler_params=pltpu.CompilerParams(
            collective_id=0, has_side_effects=True, vmem_limit_bytes=62 * 1024 * 1024
        ),
        name="tree_attention",
    )(cache_len, accept_len, parents, accept_rows, queries, tree_keys, tree_values, cache_keys, cache_values, residual, out_weight)
    return pl.pallas_call(
        write_out,
        out_shape=results,
        in_specs=[hbm] * 3,
        out_specs=(hbm, hbm, hbm),
        scratch_shapes=[
            vmem(residual.shape, bf16),
            vmem(cache_keys.shape, bf16),
            vmem(cache_values.shape, bf16),
            dma((2 * CUTS + 1,)),
            dma((2 * CUTS + 1,)),
        ],
        compiler_params=pltpu.CompilerParams(vmem_limit_bytes=62 * 1024 * 1024),
        name="write_out",
    )(*made)


def solution(mesh):
    return jax.shard_map(
        functools.partial(on_device, mesh.shape["tp"]),
        mesh=mesh,
        in_specs=(
            P("seq", None, "tp"),
            P("seq", None, "tp"),
            P("seq", None, "tp"),
            P("seq", "tp"),
            P("seq", "tp"),
            P("seq", None, "tp"),
            P("tp", None),
            P(),
            P("seq", None),
            P("seq", None),
            P(),
        ),
        out_specs=(P("seq", None, "tp"), P("seq", "tp"), P("seq", "tp")),
        check_vma=False,
    )
```
